128 devices in a mesh: group: 8 (over z, core), tensor: 16 (over y, x).
Axes of the slice: x: 4, y: 4, z: 4, core: 2. Of those that a mesh axis runs over, the one named last changes fastest.
Arguments:
- panel: bfloat16 [16384, 7168], P('group', 'tensor'), may hold values from -1.5 to 1.5, as said below
- hidden: bfloat16 [8192, 7168], P('group'), may hold values from -9 to 9
- targets: int32 [8192], P('group'), may hold values from 0 to 16383
- counts: int32 [8], P('group'), may hold values from 512 to 1024, as said below
Outputs:
- logprob: float32 [8192], P('group')
- rollout_panel: bfloat16 [16384, 7168], P('tensor')
- rollout_scale: bfloat16 [128, 56], P('tensor')
The draws below stay inside these ranges and needn't reach their ends.
Inputs may be any that keep to these rules, and one draw needn't show every extreme that they name: `counts`: live rows of one replica; at least one replica is full in every draw. `panel`: entries lie within 12 / sqrt(7168) in magnitude.
All inputs are finite; a program needn't handle non-finite values.
Results may differ from the reference program's by a relative error of at most 0.0052.
Values may be sent and summed in bfloat16 or wider, within the bound.
A program may use at most 192 MiB of HBM per device.

```python
import jax
import jax.numpy as jnp
from jax import lax

D = 7168
V_PANEL = 16384
QBLOCK = 128
ROWS = 1024
GROUPS = 8
N_GROUP = 8
N_TENSOR = 16


def base_panel(key):
    return jax.random.truncated_normal(jax.random.fold_in(key, 11), -4.0, 4.0, (V_PANEL, D), jnp.float32) * (3.0 / D ** 0.5)


def draw_panel(key, part):
    base = base_panel(key)
    return base.astype(jnp.bfloat16)


def draw_hidden(key, part):
    key = jax.random.fold_in(key, 2)
    total = ROWS * GROUPS
    values = jax.random.truncated_normal(jax.random.fold_in(key, 5), -6.0, 6.0, (total, D), jnp.float32)
    return jnp.clip(values, -9.0, 9.0).astype(jnp.bfloat16)


def draw_counts(key, part):
    key = jax.random.fold_in(key, 6)
    values = jax.random.randint(jax.random.fold_in(key, 1), (GROUPS,), ROWS // 2, ROWS + 1)
    full = jax.random.randint(jax.random.fold_in(key, 2), (), 0, GROUPS)
    return jnp.where(jnp.arange(GROUPS) == full, ROWS, values).astype(jnp.int32)


def place_ends(array, key, smallest, high):
    longest = array.shape.index(max(array.shape))
    spots = []
    for shift in (0, 1):
        where = [jax.random.randint(jax.random.fold_in(key, axis), (), 0, length) for axis, length in enumerate(array.shape)]
        where[longest] = (where[longest] + shift) % array.shape[longest]
        spots.append(tuple(where))
    return array.at[spots[0]].set(smallest).at[spots[1]].set(high)


def setup_inputs(seed: int = 0) -> dict:
    keys = jax.random.split(jax.random.key(seed), 5)
    return {
        "panel": draw_panel(jax.random.fold_in(keys[4], 71), 0),
        "hidden": draw_hidden(jax.random.fold_in(keys[4], 71), 0),
        "targets": place_ends(jax.random.randint(keys[2], (ROWS * GROUPS,), 0, V_PANEL), jax.random.fold_in(keys[2], 1), 0, V_PANEL - 1).astype(jnp.int32),
        "counts": draw_counts(jax.random.fold_in(keys[4], 71), 0),
    }


def quantize(rows):
    count, width = rows.shape
    blocks = rows.astype(jnp.float32).reshape(count // QBLOCK, QBLOCK, width // QBLOCK, QBLOCK)
    largest = jnp.max(jnp.abs(blocks), axis=(1, 3))
    scale = ((largest + 1e-6) / 448.0).astype(jnp.bfloat16)
    spread = scale.astype(jnp.float32)[:, None, :, None]
    quant = (blocks / spread).astype(jnp.bfloat16)
    held = lax.optimization_barrier(quant)
    weights = (held.astype(jnp.float32) * spread).astype(jnp.bfloat16)
    return quant.reshape(count, width), scale, weights.reshape(count, width)


def reference(panel, hidden, targets, counts):
    sub = V_PANEL // (N_GROUP * N_TENSOR)
    ordered = panel.reshape(N_GROUP, N_TENSOR, sub, D).transpose(1, 0, 2, 3).reshape(V_PANEL, D)
    quant, scale, weights = quantize(ordered)
    vocab = jnp.arange(V_PANEL, dtype=jnp.int32)
    position = ((vocab // sub) % N_TENSOR) * (N_GROUP * sub) + (vocab // (N_TENSOR * sub)) * sub + vocab % sub

    def score(items):
        states, wanted, live_count = items
        logits = jnp.dot(states, weights.T, preferred_element_type=jnp.float32)
        top = jnp.max(logits, axis=1)
        lse = top + jnp.log(jnp.sum(jnp.exp(logits - top[:, None]), axis=1))
        column = position[wanted]
        picked = jnp.take_along_axis(logits, column[:, None], axis=1)[:, 0]
        live = jnp.arange(ROWS, dtype=jnp.int32) < live_count
        return jnp.where(live, picked - lse, jnp.float32(0.0))

    result = lax.map(score, (hidden.reshape(N_GROUP, ROWS, D), targets.reshape(N_GROUP, ROWS), counts))
    return result.reshape(-1), quant, scale
```

```python
import functools

import jax
import jax.numpy as jnp
from jax import lax
from jax.experimental import pallas as pl
from jax.experimental.pallas import tpu as pltpu
from jax.sharding import PartitionSpec as P

MESH = pl.DeviceIdType.MESH
QB = 128
NZ = 4
NG = 8
NT = 16
NP = 8
ROWS = 1024
D = 7168
SRC = D // NT
CW = 2 * SRC
BLOCKS = CW // QB
HALF = QB // 2


def kernel(
    panel, hidden, targets, counts,
    logprob, quant, scale,
    arrived, states, scales, logits, stats,
    a2a_send, a2a_recv, hid_sem,
    own_send, fwd_send, core_send, sc_send, st_send,
    prev_recv, next_recv, top_recv, bot_recv, core_recv, sc_recv, st_recv,
):
    g = lax.axis_index("group")
    t = lax.axis_index("tensor")
    z, c = g // 2, g % 2
    gp = lax.rem(z + 3, NZ) * 2 + c
    gn = lax.rem(z + 1, NZ) * 2 + c
    gf = lax.rem(z + 2, NZ) * 2 + c
    go = z * 2 + 1 - c
    p0 = t // 2

    def pair(k):
        return lax.rem(p0 + k, NP)

    def cols(p):
        return pl.ds(pl.multiple_of(p * CW, CW), CW)

    def rows(b, first=0, size=QB):
        return pl.ds(pl.multiple_of(b * QB + first, HALF), size)

    def tens(u):
        return pl.ds(pl.multiple_of(u * QB, QB), QB)

    def block_of(u):
        return pl.ds(pl.multiple_of(u * SRC, SRC), SRC)

    def wait(ref, sem):
        pltpu.make_async_copy(ref, ref, sem).wait()

    def remote(src, dst, send, recv, to):
        pltpu.make_async_remote_copy(
            src_ref=src, dst_ref=dst, send_sem=send, recv_sem=recv, device_id=to, device_id_type=MESH
        ).start()

    pltpu.make_async_copy(panel.at[:, tens(t)], arrived.at[block_of(t)], a2a_recv.at[t]).start()
    barrier = pltpu.get_barrier_semaphore()

    @pl.loop(1, NT)
    def _(s):
        pl.semaphore_signal(barrier, inc=1, device_id=(g, lax.rem(t + s, NT)), device_id_type=MESH)

    @pl.loop(1, NG)
    def _(s):
        pl.semaphore_signal(barrier, inc=1, device_id=(lax.rem(g + s, NG), t), device_id_type=MESH)

    pl.semaphore_wait(barrier, NT - 1 + NG - 1)

    def send_block(u):
        remote(panel.at[:, tens(u)], arrived.at[block_of(t)], a2a_send.at[u], a2a_recv.at[t], (g, u))

    send_block(2 * p0 + 1 - lax.rem(t, 2))

    @pl.loop(1, NP)
    def _(j):
        q = lax.rem(p0 + NP - j, NP)
        send_block(2 * q)
        send_block(2 * q + 1)

    pltpu.make_async_copy(hidden, states, hid_sem).start()
    logits[...] = jnp.zeros_like(logits)

    def step_own(k):
        p = pair(k)
        wait(arrived.at[block_of(2 * p)], a2a_recv.at[2 * p])
        wait(arrived.at[block_of(2 * p + 1)], a2a_recv.at[2 * p + 1])
        lane = lax.broadcasted_iota(jnp.int32, (8, QB), 1)
        tile = jnp.zeros((8, QB), jnp.float32)
        for i in range(BLOCKS):
            block = arrived[pl.ds(pl.multiple_of(p * CW + i * QB, QB), QB)].astype(jnp.float32)
            largest = jnp.max(jnp.abs(block), axis=(0, 1), keepdims=True)
            s = ((largest + 1e-06) / 448.0).astype(jnp.bfloat16).astype(jnp.float32)
            q = (block / s).astype(jnp.bfloat16).T
            quant[rows(g), pl.ds(pl.multiple_of(p * CW + i * QB, QB), QB)] = q
            tile = jnp.where(lane == i, jnp.broadcast_to(s, (8, QB)), tile)
        scales[p, g] = tile
        block = quant.at[rows(g), cols(p)]
        remote(block, block, own_send.at[0, k], prev_recv.at[k], (gn, t))
        remote(block, block, own_send.at[1, k], next_recv.at[k], (gp, t))
        remote(block, block, core_send.at[0, k], core_recv.at[0, k], (go, t))

        @pl.loop(1, NG)
        def _(s):
            remote(scales.at[p, g], scales.at[p, g], sc_send.at[k], sc_recv.at[k], (lax.rem(g + s, NG), t))

    def step_near(k):
        p = pair(k)
        block = quant.at[rows(gp), cols(p)]
        wait(block, prev_recv.at[k])
        top = quant.at[rows(gp, 0, HALF), cols(p)]
        remote(top, top, fwd_send.at[0, k], top_recv.at[k], (gn, t))
        remote(block, block, core_send.at[1, k], core_recv.at[1, k], (go, t))
        block = quant.at[rows(gn), cols(p)]
        wait(block, next_recv.at[k])
        bot = quant.at[rows(gn, HALF, HALF), cols(p)]
        remote(bot, bot, fwd_send.at[1, k], bot_recv.at[k], (gp, t))
        remote(block, block, core_send.at[2, k], core_recv.at[2, k], (go, t))

    def step_far(k):
        p = pair(k)
        wait(quant.at[rows(gf, 0, HALF), cols(p)], top_recv.at[k])
        wait(quant.at[rows(gf, HALF, HALF), cols(p)], bot_recv.at[k])
        block = quant.at[rows(gf), cols(p)]
        remote(block, block, core_send.at[3, k], core_recv.at[3, k], (go, t))

    def step_dot(k):
        p = pair(k)
        wait(scales.at[0, pl.ds(0, NG - 1)], sc_recv.at[k])
        chunk = quant.at[rows(0), cols(p)]
        for n in range(4):
            wait(chunk, core_recv.at[n, k])

        @pl.loop(0, NZ)
        def _(j):
            b = lax.rem(z + j, NZ)
            parts = []
            for h in range(2):
                s = scales[p, 2 * b + h]
                spread = jnp.concatenate(
                    [jnp.broadcast_to(s[0:1, i:i + 1], (1, QB)) for i in range(BLOCKS)], axis=1
                )
                q = quant[rows(2 * b + h), cols(p)].astype(jnp.float32)
                parts.append((q * spread).astype(jnp.bfloat16))
            w = jnp.concatenate(parts, axis=0)
            at = pl.ds(pl.multiple_of(b * 256, 256), 256)
            logits[at, :] += lax.dot_general(
                w, states[:, cols(p)], (((1,), (1,)), ((), ())), preferred_element_type=jnp.float32
            )

    step_own(0)
    step_own(1)

    @pl.loop(0, NP + 2)
    def _(k):
        @pl.when(k < NP - 2)
        def _():
            step_own(k + 2)

        @pl.when(k < NP)
        def _():
            step_near(k)

        @pl.when(jnp.logical_and(k >= 1, k < NP + 1))
        def _():
            step_far(k - 1)

        @pl.when(k == 2)
        def _():
            pltpu.make_async_copy(hidden, states, hid_sem).wait()

        @pl.when(k >= 2)
        def _():
            step_dot(k - 2)

    row = lax.broadcasted_iota(jnp.int32, (ROWS, QB), 0)

    @pl.loop(0, 8)
    def _(j):
        x = logits[:, pl.ds(pl.multiple_of(j * QB, QB), QB)]
        v = targets[pl.ds(j, 1), :]
        mine = lax.rem(v // QB, NT) == t
        column = jnp.where(mine, v // (NT * QB) * QB + lax.rem(v, QB), -1)
        top = jnp.max(x, axis=0, keepdims=True)
        total = jnp.sum(jnp.exp(x - top), axis=0, keepdims=True)
        stats[t, 0, pl.ds(j, 1), :] = top + jnp.log(total)
        stats[t, 1, pl.ds(j, 1), :] = jnp.sum(jnp.where(row == column, x, 0.0), axis=0, keepdims=True)

    @pl.loop(1, NT)
    def _(s):
        remote(stats.at[t], stats.at[t], st_send, st_recv, (g, lax.rem(t + s, NT)))

    lane = lax.broadcasted_iota(jnp.int32, (NG, QB), 1)
    table = jnp.zeros((NG, QB), jnp.float32)
    for p in range(NP):
        v = jnp.concatenate([scales[p, b, 0:1, :] for b in range(NG)], axis=0)
        v = pltpu.roll(v, p * BLOCKS, 1) if p else v
        table = jnp.where(jnp.logical_and(lane >= p * BLOCKS, lane < (p + 1) * BLOCKS), v, table)
    scale[...] = table[:, :NP * BLOCKS].astype(jnp.bfloat16)

    @pl.loop(1, NT)
    def _(s):
        wait(panel.at[:, tens(0)], a2a_send.at[lax.rem(t + s, NT)])

    @pl.loop(0, NP)
    def _(k):
        chunk = quant.at[rows(0), cols(0)]
        half = quant.at[rows(0, 0, HALF), cols(0)]
        for n in range(2):
            wait(chunk, own_send.at[n, k])
            wait(half, fwd_send.at[n, k])
        for n in range(4):
            wait(chunk, core_send.at[n, k])
        wait(scales.at[0, pl.ds(0, NG - 1)], sc_send.at[k])

    wait(stats.at[pl.ds(0, NT - 1)], st_recv)
    lses = stats[:, 0]
    top = jnp.max(lses, axis=0)
    lse = top + jnp.log(jnp.sum(jnp.exp(lses - top[None]), axis=0))
    picked = jnp.sum(stats[:, 1], axis=0)
    token = lax.broadcasted_iota(jnp.int32, (8, QB), 0) * QB + lax.broadcasted_iota(jnp.int32, (8, QB), 1)
    logprob[...] = jnp.where(token < counts[0], picked - lse, 0.0)
    wait(stats.at[pl.ds(0, NT - 1)], st_send)


def write(held, quant, sem):
    copies = [
        pltpu.make_async_copy(held.at[pl.ds(QB * i, QB)], quant.at[pl.ds(QB * i, QB)], sem.at[i]) for i in range(8)
    ]
    for copy in copies:
        copy.start()
    for copy in copies:
        copy.wait()


def local(panel, hidden, targets, counts):
    dma = pltpu.SemaphoreType.DMA
    vmem = pl.BlockSpec(memory_space=pltpu.VMEM)
    hbm = pl.BlockSpec(memory_space=pl.ANY)
    logprob, quant, scale = pl.pallas_call(
        kernel,
        out_shape=(
            jax.ShapeDtypeStruct((8, QB), jnp.float32),
            QUANT_SHAPE,
            jax.ShapeDtypeStruct((NG, NP * BLOCKS), jnp.bfloat16),
        ),
        in_specs=[hbm, hbm, vmem, pl.BlockSpec(memory_space=pltpu.SMEM)],
        out_specs=(vmem, vmem, vmem),
        scratch_shapes=[
            pltpu.VMEM((D, QB), jnp.bfloat16),
            pltpu.VMEM((ROWS, D), jnp.bfloat16),
            pltpu.VMEM((NP, NG, 8, QB), jnp.float32),
            pltpu.VMEM((ROWS, ROWS), jnp.float32),
            pltpu.VMEM((NT, 2, 8, QB), jnp.float32),
            dma((NT,)), dma((NT,)), dma(()),
            dma((2, NP)), dma((2, NP)), dma((4, NP)), dma((NP,)), dma(()),
            dma((NP,)), dma((NP,)), dma((NP,)), dma((NP,)), dma((4, NP)), dma((NP,)), dma(()),
        ],
        compiler_params=pltpu.CompilerParams(
            collective_id=0, has_side_effects=True, vmem_limit_bytes=VMEM_LIMIT
        ),
        cost_estimate=pl.CostEstimate(flops=2 * ROWS * ROWS * D, bytes_accessed=4 * ROWS * D, transcendentals=ROWS * ROWS),
        name="refresh",
    )(panel.T, hidden, targets.reshape(8, QB), counts)
    quant = pl.pallas_call(
        write,
        out_shape=pltpu.HBM((ROWS, D), jnp.bfloat16),
        in_specs=[vmem],
        out_specs=hbm,
        scratch_shapes=[dma((8,))],
        compiler_params=pltpu.CompilerParams(vmem_limit_bytes=2 << 20),
        cost_estimate=pl.CostEstimate(flops=0, bytes_accessed=4 * ROWS * D, transcendentals=0),
        name="write",
    )(quant)
    return logprob.reshape(ROWS), quant, scale


QUANT_SHAPE = pltpu.VMEM((ROWS, D), jnp.bfloat16)
VMEM_LIMIT = 32 << 20


def solution(mesh):
    in_specs = (P("group", "tensor"), P("group", None), P("group"), P("group"))
    out_specs = (P("group"), P("tensor", None), P("tensor", None))
    return jax.shard_map(local, mesh=mesh, in_specs=in_specs, out_specs=out_specs, check_vma=False)
```

```python
import functools

import jax
import jax.numpy as jnp
from jax import lax
from jax.experimental import pallas as pl
from jax.experimental.pallas import tpu as pltpu
from jax.sharding import PartitionSpec as P

MESH = pl.DeviceIdType.MESH
QB = 128
NZ = 4
NG = 8
NT = 16
NP = 8
ROWS = 1024
D = 7168
SRC = D // NT
CW = 2 * SRC
BLOCKS = CW // QB
HALF = QB // 2
LEAD = 2
AHEAD = 4
LAG = 2
VMEM_LIMIT = 32 << 20


def kernel(
    panel, hidden, targets, counts,
    logprob, quant, scale,
    arrived, states, scales, logits, wanted, parts, stats,
    a2a_send, a2a_recv, hid_sem, tgt_sem,
    own_send, fwd_send, core_send, sc_send, st_send,
    prev_recv, next_recv, top_recv, bot_recv, core_recv, sc_recv, st_recv,
):
    g = lax.axis_index("group")
    t = lax.axis_index("tensor")
    z, c = g // 2, lax.rem(g, 2)
    gp = lax.rem(z + 3, NZ) * 2 + c
    gn = lax.rem(z + 1, NZ) * 2 + c
    gf = lax.rem(z + 2, NZ) * 2 + c
    go = z * 2 + 1 - c
    y, xh, odd = t // 4, lax.rem(t, 4) // 2, lax.rem(t, 2)

    def shift(k):
        between = jnp.logical_and(k >= 2, k < 6)
        odd_step = lax.rem(k, 2)
        return jnp.where(between, 1 + 2 * odd_step, k // 6 * 2), jnp.where(between, k // 4, odd_step)

    def pair(k):
        dy, dx = shift(k)
        return lax.rem(y + dy, 4) * 2 + lax.rem(xh + dx, 2)

    def cols(p):
        return pl.ds(pl.multiple_of(p * CW, CW), CW)

    def rows(b, first=0, size=QB):
        return pl.ds(pl.multiple_of(b * QB + first, HALF), size)

    def tens(u):
        return pl.ds(pl.multiple_of(u * QB, QB), QB)

    def block_of(u):
        return pl.ds(pl.multiple_of(u * SRC, SRC), SRC)

    def wait(ref, sem):
        pltpu.make_async_copy(ref, ref, sem).wait()

    def remote(src, dst, send, recv, to):
        pltpu.make_async_remote_copy(
            src_ref=src, dst_ref=dst, send_sem=send, recv_sem=recv, device_id=to, device_id_type=MESH
        ).start()

    pltpu.make_async_copy(panel.at[:, tens(t)], arrived.at[block_of(t)], a2a_recv.at[t]).start()
    barrier = pltpu.get_barrier_semaphore()

    @pl.loop(1, NT)
    def _(s):
        pl.semaphore_signal(barrier, inc=1, device_id=(g, lax.rem(t + s, NT)), device_id_type=MESH)

    @pl.loop(1, NG)
    def _(s):
        pl.semaphore_signal(barrier, inc=1, device_id=(lax.rem(g + s, NG), t), device_id_type=MESH)

    pltpu.make_async_copy(targets, wanted, tgt_sem).start()

    def batch(k):
        return k // 2

    def quantize(k, first, count):
        p, e = pair(k), batch(k)
        lane = lax.broadcasted_iota(jnp.int32, (8, QB), 1)
        tile = scales[e, g]
        for i in range(count):
            at = pl.multiple_of(p * CW + (first + i) * QB, QB)
            block = arrived[pl.ds(at, QB)].astype(jnp.float32)
            largest = jnp.max(jnp.abs(block), axis=(0, 1), keepdims=True)
            s = ((largest + 1e-06) / 448.0).astype(jnp.bfloat16).astype(jnp.float32)
            quant[rows(g), pl.ds(at, QB)] = (block / s).astype(jnp.bfloat16).T
            tile = jnp.where(lane == p * BLOCKS + first + i, jnp.broadcast_to(s, (8, QB)), tile)
        scales[e, g] = tile

    def send_own(k, at, width):
        block = quant.at[rows(g), pl.ds(pl.multiple_of(at, QB), width)]
        remote(block, block, own_send.at[0, k], prev_recv.at[k], (gn, t))
        remote(block, block, own_send.at[1, k], next_recv.at[k], (gp, t))
        remote(block, block, core_send.at[0, k], core_recv.at[0, k], (go, t))

    def send_scales(e):
        @pl.loop(1, NG)
        def _(s):
            remote(scales.at[e, g], scales.at[e, g], sc_send.at[e], sc_recv.at[e], (lax.rem(g + s, NG), t))

    p0 = pair(0)
    first = 4 * odd
    wait(arrived.at[block_of(t)], a2a_recv.at[t])
    for e in range(NP // 2):
        scales[e, g] = jnp.zeros((8, QB), jnp.float32)
    quantize(0, first, 3)
    logits[...] = jnp.zeros_like(logits)

    pl.semaphore_wait(barrier, NT - 1 + NG - 1)

    def send_block(u):
        remote(panel.at[:, tens(u)], arrived.at[block_of(t)], a2a_send.at[u], a2a_recv.at[t], (g, u))

    def send_pair(j):
        dy, dx = shift(j)
        q = lax.rem(y + 4 - dy, 4) * 2 + lax.rem(xh + dx, 2)
        send_block(2 * q)
        send_block(2 * q + 1)

    send_block(2 * p0 + 1 - odd)
    send_own(0, p0 * CW + first * QB, 3 * QB)
    for j in range(1, AHEAD):
        send_pair(j)
    pltpu.make_async_copy(hidden, states, hid_sem).start()

    other = 2 * p0 + 1 - odd
    wait(arrived.at[block_of(other)], a2a_recv.at[other])
    first = 3 - 3 * odd
    quantize(0, first, 4)
    send_own(0, p0 * CW + first * QB, 4 * QB)

    def step_own(k):
        p = pair(k)
        wait(arrived.at[block_of(2 * p)], a2a_recv.at[2 * p])
        wait(arrived.at[block_of(2 * p + 1)], a2a_recv.at[2 * p + 1])
        quantize(k, 0, BLOCKS)

        @pl.when(lax.rem(k, 2) == 1)
        def _():
            send_scales(batch(k))

        send_own(k, p * CW, CW)

    def step_near(k):
        p = pair(k)
        block = quant.at[rows(gp), cols(p)]
        wait(block, prev_recv.at[k])
        top = quant.at[rows(gp, 0, HALF), cols(p)]
        remote(top, top, fwd_send.at[0, k], top_recv.at[k], (gn, t))
        remote(block, block, core_send.at[1, k], core_recv.at[1, k], (go, t))
        block = quant.at[rows(gn), cols(p)]
        wait(block, next_recv.at[k])
        bot = quant.at[rows(gn, HALF, HALF), cols(p)]
        remote(bot, bot, fwd_send.at[1, k], bot_recv.at[k], (gp, t))
        remote(block, block, core_send.at[2, k], core_recv.at[2, k], (go, t))

    def step_far(k):
        p = pair(k)
        wait(quant.at[rows(gf, 0, HALF), cols(p)], top_recv.at[k])
        wait(quant.at[rows(gf, HALF, HALF), cols(p)], bot_recv.at[k])
        block = quant.at[rows(gf), cols(p)]
        remote(block, block, core_send.at[3, k], core_recv.at[3, k], (go, t))

    def dot(k, b):
        p = pair(k)
        both = []
        for h in range(2):
            s = pltpu.roll(scales[batch(k), 2 * b + h], lax.rem(QB - p * BLOCKS, QB), 1)
            spread = jnp.concatenate([jnp.broadcast_to(s[0:1, i:i + 1], (1, QB)) for i in range(BLOCKS)], axis=1)
            q = quant[rows(2 * b + h), cols(p)].astype(jnp.float32)
            both.append((q * spread).astype(jnp.bfloat16))
        w = jnp.concatenate(both, axis=0)
        at = pl.ds(pl.multiple_of(b * 256, 256), 256)
        logits[at, :] += lax.dot_general(
            w, states[:, cols(p)], (((1,), (1,)), ((), ())), preferred_element_type=jnp.float32
        )

    def dot_near(k):
        p = pair(k)
        for n in range(3):
            wait(quant.at[rows(0), cols(p)], core_recv.at[n, k])

        @pl.loop(0, 3)
        def _(j):
            dot(k, lax.rem(z + 3 + j, NZ))

    def dot_far(k):
        p = pair(k)
        wait(quant.at[rows(0), cols(p)], core_recv.at[3, k])
        dot(k, lax.rem(z + 2, NZ))

    for k in range(1, LEAD):
        send_pair(AHEAD - 1 + k)
        step_own(jnp.int32(k))

    @pl.loop(0, NP)
    def _(k):
        @pl.when(k < NP - (AHEAD - 1 + LEAD))
        def _():
            send_pair(k + AHEAD - 1 + LEAD)

        @pl.when(k < NP - LEAD)
        def _():
            step_own(k + LEAD)

        step_near(k)

        @pl.when(k >= LAG)
        def _():
            step_far(k - LAG)

        @pl.when(k == 0)
        def _():
            pltpu.make_async_copy(hidden, states, hid_sem).wait()

        @pl.when(lax.rem(k, 2) == 0)
        def _():
            wait(scales.at[0, pl.ds(0, NG - 1)], sc_recv.at[batch(k)])

        @pl.when(k < NP - 1)
        def _():
            dot_near(k)

        @pl.when(k >= LAG)
        def _():
            dot_far(k - LAG)

    row = lax.broadcasted_iota(jnp.int32, (256, QB), 0)
    pltpu.make_async_copy(targets, wanted, tgt_sem).wait()

    def measure(b):
        @pl.loop(0, 8, unroll=4)
        def _(j):
            x = logits[pl.ds(pl.multiple_of(b * 256, 256), 256), pl.ds(pl.multiple_of(j * QB, QB), QB)]
            v = wanted[pl.ds(j, 1), :]
            mine = lax.rem(v // QB, NT) == t
            column = jnp.where(mine, v // (NT * QB) * QB + lax.rem(v, QB) - b * 256, -1)
            top = jnp.max(x, axis=0, keepdims=True)
            total = jnp.sum(jnp.exp(x - top), axis=0, keepdims=True)
            parts[b, 0, pl.ds(j, 1), :] = top + jnp.log(total)
            parts[b, 1, pl.ds(j, 1), :] = jnp.sum(jnp.where(row == column, x, 0.0), axis=0, keepdims=True)

    def combine(lses):
        top = jnp.max(lses, axis=0)
        return top + jnp.log(jnp.sum(jnp.exp(lses - top[None]), axis=0))

    for k in range(NP - LAG, NP):
        if k == NP - 1:
            @pl.loop(0, 3)
            def _(j):
                measure(lax.rem(z + 3 + j, NZ))

        step_far(k)
        if k == NP - LAG:
            dot_near(NP - 1)
        dot_far(k)

    measure(lax.rem(z + 2, NZ))
    stats[t, 0] = combine(parts[:, 0])
    stats[t, 1] = jnp.sum(parts[:, 1], axis=0)

    @pl.loop(1, NT)
    def _(s):
        remote(stats.at[t], stats.at[t], st_send, st_recv, (g, lax.rem(t + s, NT)))

    table = jnp.concatenate([jnp.sum(scales[:, b, 0:1, :], axis=0) for b in range(NG)], axis=0)
    scale[...] = table[:, :NP * BLOCKS].astype(jnp.bfloat16)

    @pl.loop(1, NT)
    def _(s):
        wait(panel.at[:, tens(0)], a2a_send.at[lax.rem(t + s, NT)])

    @pl.loop(0, NP)
    def _(k):
        chunk = quant.at[rows(0), cols(0)]
        half = quant.at[rows(0, 0, HALF), cols(0)]
        for n in range(2):
            wait(chunk, own_send.at[n, k])
            wait(half, fwd_send.at[n, k])
        for n in range(4):
            wait(chunk, core_send.at[n, k])

    for e in range(NP // 2):
        wait(scales.at[0, pl.ds(0, NG - 1)], sc_send.at[e])

    wait(stats.at[pl.ds(0, NT - 1)], st_recv)
    token = lax.broadcasted_iota(jnp.int32, (8, QB), 0) * QB + lax.broadcasted_iota(jnp.int32, (8, QB), 1)
    gap = jnp.sum(stats[:, 1], axis=0) - combine(stats[:, 0])
    logprob[...] = jnp.where(token < counts[0], gap, 0.0)
    wait(stats.at[pl.ds(0, NT - 1)], st_send)


def write(held, held_logprob, held_scale, quant, logprob, scale, sem):
    copies = [
        pltpu.make_async_copy(held.at[pl.ds(QB * i, QB)], quant.at[pl.ds(QB * i, QB)], sem.at[i]) for i in range(8)
    ]
    copies.append(pltpu.make_async_copy(held_logprob, logprob, sem.at[8]))
    copies.append(pltpu.make_async_copy(held_scale, scale, sem.at[9]))
    for copy in copies:
        copy.start()
    for copy in copies:
        copy.wait()


def local(panel, hidden, targets, counts):
    dma = pltpu.SemaphoreType.DMA
    vmem = pl.BlockSpec(memory_space=pltpu.VMEM)
    hbm = pl.BlockSpec(memory_space=pltpu.HBM)
    held = pl.pallas_call(
        kernel,
        out_shape=(
            pltpu.VMEM((8, QB), jnp.float32),
            pltpu.VMEM((ROWS, D), jnp.bfloat16),
            pltpu.VMEM((NG, NP * BLOCKS), jnp.bfloat16),
        ),
        in_specs=[hbm, hbm, hbm, pl.BlockSpec(memory_space=pltpu.SMEM)],
        out_specs=(vmem, vmem, vmem),
        scratch_shapes=[
            pltpu.VMEM((D, QB), jnp.bfloat16),
            pltpu.VMEM((ROWS, D), jnp.bfloat16),
            pltpu.VMEM((NP // 2, NG, 8, QB), jnp.float32),
            pltpu.VMEM((ROWS, ROWS), jnp.float32),
            pltpu.VMEM((8, QB), jnp.int32),
            pltpu.VMEM((NZ, 2, 8, QB), jnp.float32),
            pltpu.VMEM((NT, 2, 8, QB), jnp.float32),
            dma((NT,)), dma((NT,)), dma(()), dma(()),
            dma((2, NP)), dma((2, NP)), dma((4, NP)), dma((NP // 2,)), dma(()),
            dma((NP,)), dma((NP,)), dma((NP,)), dma((NP,)), dma((4, NP)), dma((NP // 2,)), dma(()),
        ],
        compiler_params=pltpu.CompilerParams(
            collective_id=0, has_side_effects=True, vmem_limit_bytes=VMEM_LIMIT
        ),
        cost_estimate=pl.CostEstimate(
            flops=2 * ROWS * ROWS * D, bytes_accessed=4 * ROWS * D, transcendentals=ROWS * ROWS
        ),
        name="refresh",
    )(
        pltpu.with_memory_space_constraint(panel.T, pltpu.HBM),
        hidden,
        pltpu.with_memory_space_constraint(targets.reshape(8, QB), pltpu.HBM),
        counts,
    )
    quant, logprob, scale = pl.pallas_call(
        write,
        out_shape=(
            pltpu.HBM((ROWS, D), jnp.bfloat16),
            pltpu.HBM((8, QB), jnp.float32),
            pltpu.HBM((NG, NP * BLOCKS), jnp.bfloat16),
        ),
        in_specs=[vmem] * 3,
        out_specs=(hbm,) * 3,
        scratch_shapes=[dma((10,))],
        compiler_params=pltpu.CompilerParams(vmem_limit_bytes=2 << 20),
        cost_estimate=pl.CostEstimate(flops=0, bytes_accessed=4 * ROWS * D, transcendentals=0),
        name="write",
    )(held[1], held[0], held[2])
    return logprob.reshape(ROWS), quant, scale


def solution(mesh):
    in_specs = (P("group", "tensor"), P("group", None), P("group"), P("group"))
    out_specs = (P("group"), P("tensor", None), P("tensor", None))
    return jax.shard_map(local, mesh=mesh, in_specs=in_specs, out_specs=out_specs, check_vma=False)
```

```python
import functools

import jax
import jax.numpy as jnp
from jax import lax
from jax.experimental import pallas as pl
from jax.experimental.pallas import tpu as pltpu
from jax.sharding import PartitionSpec as P

MESH = pl.DeviceIdType.MESH
QB = 128
NZ = 4
NG = 8
NT = 16
NP = 8
ROWS = 1024
D = 7168
SRC = D // NT
CW = 2 * SRC
BLOCKS = CW // QB
HALF = QB // 2
LEAD = 2
AHEAD = 4
LAG = 2
VMEM_LIMIT = 32 << 20


def kernel(
    panel, hidden, targets, counts,
    logprob, quant, scale,
    arrived, states, scales, logits, wanted, parts, stats,
    a2a_send, a2a_recv, hid_sem, tgt_sem, near_recv, near_send,
    own_send, fwd_send, core_send, sc_send, st_send,
    prev_recv, next_recv, top_recv, bot_recv, core_recv, sc_recv, st_recv,
):
    g = lax.axis_index("group")
    t = lax.axis_index("tensor")
    z, c = g // 2, lax.rem(g, 2)
    gp = lax.rem(z + 3, NZ) * 2 + c
    gn = lax.rem(z + 1, NZ) * 2 + c
    gf = lax.rem(z + 2, NZ) * 2 + c
    go = z * 2 + 1 - c
    y, xh, odd = t // 4, lax.rem(t, 4) // 2, lax.rem(t, 2)

    def shift(k):
        r = lax.rem(k, 3)
        return jnp.where(k < 6, r + r // 2, 2), jnp.where(k < 6, k // 3, k - 6)

    def pair(k):
        dy, dx = shift(k)
        return lax.rem(y + dy, 4) * 2 + lax.rem(xh + dx, 2)

    def cols(p):
        return pl.ds(pl.multiple_of(p * CW, CW), CW)

    def rows(b, first=0, size=QB):
        return pl.ds(pl.multiple_of(b * QB + first, HALF), size)

    def tens(u):
        return pl.ds(pl.multiple_of(u * QB, QB), QB)

    def block_of(u):
        return pl.ds(pl.multiple_of(u * SRC, SRC), SRC)

    def wait(ref, sem):
        pltpu.make_async_copy(ref, ref, sem).wait()

    def remote(src, dst, send, recv, to):
        pltpu.make_async_remote_copy(
            src_ref=src, dst_ref=dst, send_sem=send, recv_sem=recv, device_id=to, device_id_type=MESH
        ).start()

    pltpu.make_async_copy(panel.at[:, tens(t)], arrived.at[block_of(t)], a2a_recv.at[t]).start()
    barrier = pltpu.get_barrier_semaphore()
    p0 = pair(0)

    @pl.loop(1, NT)
    def _(s):
        pl.semaphore_signal(barrier, inc=1, device_id=(g, lax.rem(t + s, NT)), device_id_type=MESH)

    @pl.loop(1, NG)
    def _(s):
        pl.semaphore_signal(barrier, inc=1, device_id=(lax.rem(g + s, NG), t), device_id_type=MESH)

    pltpu.make_async_copy(targets, wanted, tgt_sem).start()

    def batch(k):
        return k // 2

    def quantize(k, first, count):
        p, e = pair(k), batch(k)
        lane = lax.broadcasted_iota(jnp.int32, (1, QB), 1)
        tile = scales[e, g]
        for i in range(count):
            at = pl.multiple_of(p * CW + (first + i) * QB, QB)
            block = arrived[pl.ds(at, QB)].astype(jnp.float32)
            largest = jnp.max(jnp.abs(block), axis=(0, 1), keepdims=True)
            s = ((largest + 1e-06) / 448.0).astype(jnp.bfloat16).astype(jnp.float32)
            quant[rows(g), pl.ds(at, QB)] = (block / s).astype(jnp.bfloat16).T
            tile = jnp.where(lane == p * BLOCKS + first + i, jnp.broadcast_to(s, (1, QB)), tile)
        scales[e, g] = tile

    def send_own(k, at, width):
        block = quant.at[rows(g), pl.ds(pl.multiple_of(at, QB), width)]
        remote(block, block, own_send.at[0, k], prev_recv.at[k], (gn, t))
        remote(block, block, own_send.at[1, k], next_recv.at[k], (gp, t))
        remote(block, block, core_send.at[0, k], core_recv.at[0, k], (go, t))

    def send_scales(e):
        @pl.loop(1, NG)
        def _(s):
            remote(scales.at[e, g], scales.at[e, g], sc_send.at[e], sc_recv.at[e], (lax.rem(g + s, NG), t))

    pl.semaphore_wait(barrier, NT - 1 + NG - 1)

    def send_block(u):
        remote(panel.at[:, tens(u)], arrived.at[block_of(t)], a2a_send.at[u], a2a_recv.at[t], (g, u))

    def send_pair(j):
        dy, dx = shift(j)
        q = lax.rem(y + 4 - dy, 4) * 2 + lax.rem(xh + dx, 2)
        send_block(2 * q)
        send_block(2 * q + 1)

    other = 2 * p0 + 1 - odd
    edge = HALF + QB

    def columns(u, at, size):
        return pl.ds(pl.multiple_of(u * SRC + at, HALF), size)

    def near_part(u, side, first):
        at = (SRC - edge) * (1 - side) if first else edge * side
        return at, (edge if first else SRC - edge)

    for part in (True, False):
        at, size = near_part(t, odd, part)
        remote(
            panel.at[pl.ds(pl.multiple_of(at, HALF), size), tens(other)],
            arrived.at[columns(t, at, size)],
            near_send if part else a2a_send.at[other],
            near_recv if part else a2a_recv.at[t],
            (g, other),
        )

    for e in range(NP // 2):
        scales[e, g] = jnp.zeros((1, QB), jnp.float32)
    wait(arrived.at[block_of(t)], a2a_recv.at[t])
    quantize(0, 4 * odd, 3)
    send_own(0, p0 * CW + 4 * odd * QB, 3 * QB)
    for j in range(1, AHEAD):
        send_pair(j)
    pltpu.make_async_copy(hidden, states, hid_sem).start()
    logits[...] = jnp.zeros_like(logits)

    for part in (True, False):
        at, size = near_part(other, 1 - odd, part)
        wait(arrived.at[columns(other, at, size)], near_recv if part else a2a_recv.at[other])
        first = (3 - 1 * odd) if part else (5 - 5 * odd)
        quantize(0, first, 2)
        send_own(0, p0 * CW + first * QB, 2 * QB)

    def step_own(k):
        p = pair(k)
        wait(arrived.at[block_of(2 * p)], a2a_recv.at[2 * p])
        wait(arrived.at[block_of(2 * p + 1)], a2a_recv.at[2 * p + 1])
        quantize(k, 0, BLOCKS)

        @pl.when(lax.rem(k, 2) == 1)
        def _():
            send_scales(batch(k))

        send_own(k, p * CW, CW)

    def step_near(k):
        p = pair(k)
        block = quant.at[rows(gp), cols(p)]
        wait(block, prev_recv.at[k])
        top = quant.at[rows(gp, 0, HALF), cols(p)]
        remote(top, top, fwd_send.at[0, k], top_recv.at[k], (gn, t))
        remote(block, block, core_send.at[1, k], core_recv.at[1, k], (go, t))
        block = quant.at[rows(gn), cols(p)]
        wait(block, next_recv.at[k])
        bot = quant.at[rows(gn, HALF, HALF), cols(p)]
        remote(bot, bot, fwd_send.at[1, k], bot_recv.at[k], (gp, t))
        remote(block, block, core_send.at[2, k], core_recv.at[2, k], (go, t))

    def step_far(k):
        p = pair(k)
        wait(quant.at[rows(gf, 0, HALF), cols(p)], top_recv.at[k])
        wait(quant.at[rows(gf, HALF, HALF), cols(p)], bot_recv.at[k])
        block = quant.at[rows(gf), cols(p)]
        remote(block, block, core_send.at[3, k], core_recv.at[3, k], (go, t))

    def dot(k, b):
        p = pair(k)
        both = []
        for h in range(2):
            s = pltpu.roll(scales[batch(k), 2 * b + h], lax.rem(QB - p * BLOCKS, QB), 1)
            spread = jnp.concatenate([jnp.broadcast_to(s[0:1, i:i + 1], (1, QB)) for i in range(BLOCKS)], axis=1)
            q = quant[rows(2 * b + h), cols(p)].astype(jnp.float32)
            both.append((q * spread).astype(jnp.bfloat16))
        w = jnp.concatenate(both, axis=0)
        at = pl.ds(pl.multiple_of(b * 256, 256), 256)
        logits[at, :] += lax.dot_general(
            w, states[:, cols(p)], (((1,), (1,)), ((), ())), preferred_element_type=jnp.float32
        )

    def dot_near(k):
        p = pair(k)
        for n in range(3):
            wait(quant.at[rows(0), cols(p)], core_recv.at[n, k])

        @pl.loop(0, 3)
        def _(j):
            dot(k, lax.rem(z + 3 + j, NZ))

    def dot_far(k):
        p = pair(k)
        wait(quant.at[rows(0), cols(p)], core_recv.at[3, k])
        dot(k, lax.rem(z + 2, NZ))

    p1 = pair(1)
    for first, count in ((0, 3), (3, 4)):
        source = 2 * p1 + first // 3
        wait(arrived.at[block_of(source)], a2a_recv.at[source])
        quantize(1, first, count)
        if first:
            send_scales(0)
        send_own(1, p1 * CW + first * QB, count * QB)
    send_pair(AHEAD)

    @pl.loop(0, NP)
    def _(k):
        @pl.when(k < NP - (AHEAD - 1 + LEAD))
        def _():
            send_pair(k + AHEAD - 1 + LEAD)

        @pl.when(k < NP - LEAD)
        def _():
            step_own(k + LEAD)

        step_near(k)

        @pl.when(k == 0)
        def _():
            pltpu.make_async_copy(hidden, states, hid_sem).wait()

        @pl.when(lax.rem(k, 2) == 0)
        def _():
            wait(scales.at[0, pl.ds(0, NG - 1)], sc_recv.at[batch(k)])

        dot_near(k)

        @pl.when(k >= LAG)
        def _():
            step_far(k - LAG)
            dot_far(k - LAG)

    row = lax.broadcasted_iota(jnp.int32, (256, QB), 0)
    pltpu.make_async_copy(targets, wanted, tgt_sem).wait()

    def measure(b):
        @pl.loop(0, 8, unroll=4)
        def _(j):
            x = logits[pl.ds(pl.multiple_of(b * 256, 256), 256), pl.ds(pl.multiple_of(j * QB, QB), QB)]
            v = wanted[pl.ds(j, 1), :]
            mine = lax.rem(v // QB, NT) == t
            column = jnp.where(mine, v // (NT * QB) * QB + lax.rem(v, QB) - b * 256, -1)
            top = jnp.max(x, axis=0, keepdims=True)
            total = jnp.sum(jnp.exp(x - top), axis=0, keepdims=True)
            parts[b, 0, pl.ds(j, 1), :] = top + jnp.log(total)
            parts[b, 1, pl.ds(j, 1), :] = jnp.sum(jnp.where(row == column, x, 0.0), axis=0, keepdims=True)

    def combine(lses):
        top = jnp.max(lses, axis=0)
        return top + jnp.log(jnp.sum(jnp.exp(lses - top[None]), axis=0))

    step_far(NP - 2)

    @pl.loop(0, 3)
    def _(j):
        measure(lax.rem(z + 3 + j, NZ))

    step_far(NP - 1)
    dot_far(NP - 2)
    dot_far(NP - 1)
    measure(lax.rem(z + 2, NZ))
    stats[t, 0] = combine(parts[:, 0])
    stats[t, 1] = jnp.sum(parts[:, 1], axis=0)

    @pl.loop(1, NT)
    def _(s):
        remote(stats.at[t], stats.at[t], st_send, st_recv, (g, lax.rem(t + s, NT)))

    table = jnp.concatenate([jnp.sum(scales[:, b], axis=0) for b in range(NG)], axis=0)
    scale[...] = table[:, :NP * BLOCKS].astype(jnp.bfloat16)

    wait(panel.at[pl.ds(0, edge), tens(0)], near_send)
    wait(panel.at[pl.ds(0, SRC - edge), tens(0)], a2a_send.at[other])

    @pl.loop(1, NP)
    def _(j):
        q = lax.rem(p0 + j, NP)
        wait(panel.at[:, tens(0)], a2a_send.at[2 * q])
        wait(panel.at[:, tens(0)], a2a_send.at[2 * q + 1])

    @pl.loop(0, NP)
    def _(k):
        chunk = quant.at[rows(0), cols(0)]
        half = quant.at[rows(0, 0, HALF), cols(0)]
        for n in range(2):
            wait(chunk, own_send.at[n, k])
            wait(half, fwd_send.at[n, k])
        for n in range(4):
            wait(chunk, core_send.at[n, k])

    for e in range(NP // 2):
        wait(scales.at[0, pl.ds(0, NG - 1)], sc_send.at[e])

    wait(stats.at[pl.ds(0, NT - 1)], st_recv)
    token = lax.broadcasted_iota(jnp.int32, (8, QB), 0) * QB + lax.broadcasted_iota(jnp.int32, (8, QB), 1)
    gap = jnp.sum(stats[:, 1], axis=0) - combine(stats[:, 0])
    logprob[...] = jnp.where(token < counts[0], gap, 0.0)
    wait(stats.at[pl.ds(0, NT - 1)], st_send)


def write(held, held_logprob, held_scale, quant, logprob, scale, sem):
    copies = [
        pltpu.make_async_copy(held.at[pl.ds(QB * i, QB)], quant.at[pl.ds(QB * i, QB)], sem.at[i]) for i in range(8)
    ]
    copies.append(pltpu.make_async_copy(held_logprob, logprob, sem.at[8]))
    copies.append(pltpu.make_async_copy(held_scale, scale, sem.at[9]))
    for copy in copies:
        copy.start()
    for copy in copies:
        copy.wait()


def local(panel, hidden, targets, counts):
    dma = pltpu.SemaphoreType.DMA
    vmem = pl.BlockSpec(memory_space=pltpu.VMEM)
    hbm = pl.BlockSpec(memory_space=pltpu.HBM)
    held = pl.pallas_call(
        kernel,
        out_shape=(
            pltpu.VMEM((8, QB), jnp.float32),
            pltpu.VMEM((ROWS, D), jnp.bfloat16),
            pltpu.VMEM((NG, NP * BLOCKS), jnp.bfloat16),
        ),
        in_specs=[hbm, hbm, hbm, pl.BlockSpec(memory_space=pltpu.SMEM)],
        out_specs=(vmem, vmem, vmem),
        scratch_shapes=[
            pltpu.VMEM((D, QB), jnp.bfloat16),
            pltpu.VMEM((ROWS, D), jnp.bfloat16),
            pltpu.VMEM((NP // 2, NG, 1, QB), jnp.float32),
            pltpu.VMEM((ROWS, ROWS), jnp.float32),
            pltpu.VMEM((8, QB), jnp.int32),
            pltpu.VMEM((NZ, 2, 8, QB), jnp.float32),
            pltpu.VMEM((NT, 2, 8, QB), jnp.float32),
            dma((NT,)), dma((NT,)), dma(()), dma(()), dma(()), dma(()),
            dma((2, NP)), dma((2, NP)), dma((4, NP)), dma((NP // 2,)), dma(()),
            dma((NP,)), dma((NP,)), dma((NP,)), dma((NP,)), dma((4, NP)), dma((NP // 2,)), dma(()),
        ],
        compiler_params=pltpu.CompilerParams(
            collective_id=0, has_side_effects=True, vmem_limit_bytes=VMEM_LIMIT
        ),
        cost_estimate=pl.CostEstimate(
            flops=2 * ROWS * ROWS * D, bytes_accessed=4 * ROWS * D, transcendentals=ROWS * ROWS
        ),
        name="refresh",
    )(
        pltpu.with_memory_space_constraint(panel.T, pltpu.HBM),
        hidden,
        pltpu.with_memory_space_constraint(targets.reshape(8, QB), pltpu.HBM),
        counts,
    )
    quant, logprob, scale = pl.pallas_call(
        write,
        out_shape=(
            pltpu.HBM((ROWS, D), jnp.bfloat16),
            pltpu.HBM((8, QB), jnp.float32),
            pltpu.HBM((NG, NP * BLOCKS), jnp.bfloat16),
        ),
        in_specs=[vmem] * 3,
        out_specs=(hbm,) * 3,
        scratch_shapes=[dma((10,))],
        compiler_params=pltpu.CompilerParams(vmem_limit_bytes=2 << 20),
        cost_estimate=pl.CostEstimate(flops=0, bytes_accessed=4 * ROWS * D, transcendentals=0),
        name="write",
    )(held[1], held[0], held[2])
    return logprob.reshape(ROWS), quant, scale


def solution(mesh):
    in_specs = (P("group", "tensor"), P("group", None), P("group"), P("group"))
    out_specs = (P("group"), P("tensor", None), P("tensor", None))
    return jax.shard_map(local, mesh=mesh, in_specs=in_specs, out_specs=out_specs, check_vma=False)
```

```python
import functools

import jax
import jax.numpy as jnp
from jax import lax
from jax.experimental import pallas as pl
from jax.experimental.pallas import tpu as pltpu
from jax.sharding import PartitionSpec as P

MESH = pl.DeviceIdType.MESH
QB = 128
NZ = 4
NG = 8
NT = 16
NP = 8
ROWS = 1024
D = 7168
SRC = D // NT
CW = 2 * SRC
BLOCKS = CW // QB
HALF = QB // 2
LEAD = 2
AHEAD = 4
LAG = 2
VMEM_LIMIT = 32 << 20


def kernel(
    panel, hidden, targets, counts,
    logprob, quant, scale,
    arrived, states, scales, logits, wanted, parts, stats,
    a2a_send, a2a_recv, hid_sem, tgt_sem, near_recv, near_send,
    own_send, fwd_send, core_send, sc_send, st_send,
    prev_recv, next_recv, top_recv, bot_recv, core_recv, sc_recv, st_recv,
):
    g = lax.axis_index("group")
    t = lax.axis_index("tensor")
    z, c = g // 2, lax.rem(g, 2)
    gp = lax.rem(z + 3, NZ) * 2 + c
    gn = lax.rem(z + 1, NZ) * 2 + c
    gf = lax.rem(z + 2, NZ) * 2 + c
    go = z * 2 + 1 - c
    y, xh, odd = t // 4, lax.rem(t, 4) // 2, lax.rem(t, 2)

    def shift(k):
        def among(*steps):
            return functools.reduce(jnp.logical_or, [k == n for n in steps])

        dy = jnp.where(among(1, 4), 1, jnp.where(among(3, 5), 3, jnp.where(k >= 6, 2, 0)))
        return dy, jnp.where(among(2, 4, 5, 7), 1, 0)

    def pair(k):
        dy, dx = shift(k)
        return lax.rem(y + dy, 4) * 2 + lax.rem(xh + dx, 2)

    def cols(p):
        return pl.ds(pl.multiple_of(p * CW, CW), CW)

    def rows(b, first=0, size=QB):
        return pl.ds(pl.multiple_of(b * QB + first, HALF), size)

    def tens(u):
        return pl.ds(pl.multiple_of(u * QB, QB), QB)

    def block_of(u):
        return pl.ds(pl.multiple_of(u * SRC, SRC), SRC)

    def wait(ref, sem):
        pltpu.make_async_copy(ref, ref, sem).wait()

    def remote(src, dst, send, recv, to):
        pltpu.make_async_remote_copy(
            src_ref=src, dst_ref=dst, send_sem=send, recv_sem=recv, device_id=to, device_id_type=MESH
        ).start()

    pltpu.make_async_copy(panel.at[:, tens(t)], arrived.at[block_of(t)], a2a_recv.at[t]).start()
    barrier = pltpu.get_barrier_semaphore()
    p0 = pair(0)

    @pl.loop(1, NT)
    def _(s):
        pl.semaphore_signal(barrier, inc=1, device_id=(g, lax.rem(t + s, NT)), device_id_type=MESH)

    @pl.loop(1, NG)
    def _(s):
        pl.semaphore_signal(barrier, inc=1, device_id=(lax.rem(g + s, NG), t), device_id_type=MESH)

    pltpu.make_async_copy(targets, wanted, tgt_sem).start()

    def batch(k):
        return k // 2

    def quantize(k, first, count):
        p, e = pair(k), batch(k)
        lane = lax.broadcasted_iota(jnp.int32, (1, QB), 1)
        tile = scales[e, g]
        for i in range(count):
            at = pl.multiple_of(p * CW + (first + i) * QB, QB)
            block = arrived[pl.ds(at, QB)].astype(jnp.float32)
            largest = jnp.max(jnp.abs(block), axis=(0, 1), keepdims=True)
            s = ((largest + 1e-06) / 448.0).astype(jnp.bfloat16).astype(jnp.float32)
            quant[rows(g), pl.ds(at, QB)] = (block / s).astype(jnp.bfloat16).T
            tile = jnp.where(lane == p * BLOCKS + first + i, jnp.broadcast_to(s, (1, QB)), tile)
        scales[e, g] = tile

    def send_own(k, at, width):
        block = quant.at[rows(g), pl.ds(pl.multiple_of(at, QB), width)]
        remote(block, block, own_send.at[0, k], prev_recv.at[k], (gn, t))
        remote(block, block, own_send.at[1, k], next_recv.at[k], (gp, t))
        remote(block, block, core_send.at[0, k], core_recv.at[0, k], (go, t))

    def send_scales(e):
        @pl.loop(1, NG)
        def _(s):
            remote(scales.at[e, g], scales.at[e, g], sc_send.at[e], sc_recv.at[e], (lax.rem(g + s, NG), t))

    pl.semaphore_wait(barrier, NT - 1 + NG - 1)

    def send_block(u):
        remote(panel.at[:, tens(u)], arrived.at[block_of(t)], a2a_send.at[u], a2a_recv.at[t], (g, u))

    def send_pair(j):
        dy, dx = shift(j)
        q = lax.rem(y + 4 - dy, 4) * 2 + lax.rem(xh + dx, 2)
        send_block(2 * q)
        send_block(2 * q + 1)

    other = 2 * p0 + 1 - odd
    edge = HALF + QB

    def columns(u, at, size):
        return pl.ds(pl.multiple_of(u * SRC + at, HALF), size)

    def near_part(u, side, first):
        at = (SRC - edge) * (1 - side) if first else edge * side
        return at, (edge if first else SRC - edge)

    for part in (True, False):
        at, size = near_part(t, odd, part)
        remote(
            panel.at[pl.ds(pl.multiple_of(at, HALF), size), tens(other)],
            arrived.at[columns(t, at, size)],
            near_send if part else a2a_send.at[other],
            near_recv if part else a2a_recv.at[t],
            (g, other),
        )

    for e in range(NP // 2):
        scales[e, g] = jnp.zeros((1, QB), jnp.float32)
    wait(arrived.at[block_of(t)], a2a_recv.at[t])
    quantize(0, 4 * odd, 3)
    send_own(0, p0 * CW + 4 * odd * QB, 3 * QB)
    for j in range(1, AHEAD):
        send_pair(j)
    pltpu.make_async_copy(hidden, states, hid_sem).start()
    logits[...] = jnp.zeros_like(logits)

    for part in (True, False):
        at, size = near_part(other, 1 - odd, part)
        wait(arrived.at[columns(other, at, size)], near_recv if part else a2a_recv.at[other])
        first = (3 - 1 * odd) if part else (5 - 5 * odd)
        quantize(0, first, 2)
        send_own(0, p0 * CW + first * QB, 2 * QB)

    def step_own(k):
        p = pair(k)
        wait(arrived.at[block_of(2 * p)], a2a_recv.at[2 * p])
        wait(arrived.at[block_of(2 * p + 1)], a2a_recv.at[2 * p + 1])
        quantize(k, 0, BLOCKS)

        @pl.when(lax.rem(k, 2) == 1)
        def _():
            send_scales(batch(k))

        send_own(k, p * CW, CW)

    def step_near(k):
        p = pair(k)
        block = quant.at[rows(gp), cols(p)]
        wait(block, prev_recv.at[k])
        top = quant.at[rows(gp, 0, HALF), cols(p)]
        remote(top, top, fwd_send.at[0, k], top_recv.at[k], (gn, t))
        remote(block, block, core_send.at[1, k], core_recv.at[1, k], (go, t))
        block = quant.at[rows(gn), cols(p)]
        wait(block, next_recv.at[k])
        bot = quant.at[rows(gn, HALF, HALF), cols(p)]
        remote(bot, bot, fwd_send.at[1, k], bot_recv.at[k], (gp, t))
        remote(block, block, core_send.at[2, k], core_recv.at[2, k], (go, t))

    def step_far(k):
        p = pair(k)
        wait(quant.at[rows(gf, 0, HALF), cols(p)], top_recv.at[k])
        wait(quant.at[rows(gf, HALF, HALF), cols(p)], bot_recv.at[k])
        block = quant.at[rows(gf), cols(p)]
        remote(block, block, core_send.at[3, k], core_recv.at[3, k], (go, t))

    def dot(k, b):
        p = pair(k)
        both = []
        for h in range(2):
            s = pltpu.roll(scales[batch(k), 2 * b + h], lax.rem(QB - p * BLOCKS, QB), 1)
            spread = jnp.concatenate([jnp.broadcast_to(s[0:1, i:i + 1], (1, QB)) for i in range(BLOCKS)], axis=1)
            q = quant[rows(2 * b + h), cols(p)].astype(jnp.float32)
            both.append((q * spread).astype(jnp.bfloat16))
        w = jnp.concatenate(both, axis=0)
        at = pl.ds(pl.multiple_of(b * 256, 256), 256)
        logits[at, :] += lax.dot_general(
            w, states[:, cols(p)], (((1,), (1,)), ((), ())), preferred_element_type=jnp.float32
        )

    def dot_own(k):
        wait(quant.at[rows(0), cols(0)], core_recv.at[0, k])
        dot(k, z)

    def dot_near(k):
        for n in range(1, 3):
            wait(quant.at[rows(0), cols(0)], core_recv.at[n, k])

        @pl.loop(0, 2)
        def _(j):
            dot(k, lax.rem(z + 1 + 2 * j, NZ))

    def dot_far(k):
        wait(quant.at[rows(0), cols(0)], core_recv.at[3, k])
        dot(k, lax.rem(z + 2, NZ))

    p1 = pair(1)
    for first, count in ((0, 3), (3, 4)):
        source = 2 * p1 + first // 3
        wait(arrived.at[block_of(source)], a2a_recv.at[source])
        quantize(1, first, count)
        if first:
            send_scales(0)
        send_own(1, p1 * CW + first * QB, count * QB)
    send_pair(AHEAD)
    for k in range(2, LEAD):
        send_pair(AHEAD - 1 + k)
        step_own(jnp.int32(k))

    @pl.loop(0, NP)
    def _(k):
        @pl.when(k < NP - (AHEAD - 1 + LEAD))
        def _():
            send_pair(k + AHEAD - 1 + LEAD)

        @pl.when(k < NP - LEAD)
        def _():
            step_own(k + LEAD)

        @pl.when(lax.rem(k, 2) == 1)
        def _():
            dot_own(k)

        step_near(k)

        @pl.when(k >= LAG)
        def _():
            step_far(k - LAG)

        @pl.when(k == 0)
        def _():
            pltpu.make_async_copy(hidden, states, hid_sem).wait()

        @pl.when(lax.rem(k, 2) == 0)
        def _():
            wait(scales.at[0, pl.ds(0, NG - 1)], sc_recv.at[batch(k)])
            dot_own(k)

        dot_near(k)

        @pl.when(k >= LAG)
        def _():
            dot_far(k - LAG)

    row = lax.broadcasted_iota(jnp.int32, (256, QB), 0)
    pltpu.make_async_copy(targets, wanted, tgt_sem).wait()

    def measure(b):
        @pl.loop(0, 8, unroll=4)
        def _(j):
            x = logits[pl.ds(pl.multiple_of(b * 256, 256), 256), pl.ds(pl.multiple_of(j * QB, QB), QB)]
            v = wanted[pl.ds(j, 1), :]
            mine = lax.rem(v // QB, NT) == t
            column = jnp.where(mine, v // (NT * QB) * QB + lax.rem(v, QB) - b * 256, -1)
            top = jnp.max(x, axis=0, keepdims=True)
            total = jnp.sum(jnp.exp(x - top), axis=0, keepdims=True)
            parts[b, 0, pl.ds(j, 1), :] = top + jnp.log(total)
            parts[b, 1, pl.ds(j, 1), :] = jnp.sum(jnp.where(row == column, x, 0.0), axis=0, keepdims=True)

    def combine(lses):
        top = jnp.max(lses, axis=0)
        return top + jnp.log(jnp.sum(jnp.exp(lses - top[None]), axis=0))

    for k in range(NP - LAG, NP - 2):
        step_far(k)
        dot_far(k)

    step_far(NP - 2)

    @pl.loop(0, 3)
    def _(j):
        measure(lax.rem(z + 3 + j, NZ))

    step_far(NP - 1)
    dot_far(NP - 2)
    dot_far(NP - 1)
    measure(lax.rem(z + 2, NZ))
    stats[t, 0] = combine(parts[:, 0])
    stats[t, 1] = jnp.sum(parts[:, 1], axis=0)

    @pl.loop(1, NT)
    def _(s):
        remote(stats.at[t], stats.at[t], st_send, st_recv, (g, lax.rem(t + s, NT)))

    table = jnp.concatenate([jnp.sum(scales[:, b], axis=0) for b in range(NG)], axis=0)
    scale[...] = table[:, :NP * BLOCKS].astype(jnp.bfloat16)

    wait(panel.at[pl.ds(0, edge), tens(0)], near_send)
    wait(panel.at[pl.ds(0, SRC - edge), tens(0)], a2a_send.at[other])

    @pl.loop(1, NP)
    def _(j):
        q = lax.rem(p0 + j, NP)
        wait(panel.at[:, tens(0)], a2a_send.at[2 * q])
        wait(panel.at[:, tens(0)], a2a_send.at[2 * q + 1])

    @pl.loop(0, NP)
    def _(k):
        chunk = quant.at[rows(0), cols(0)]
        half = quant.at[rows(0, 0, HALF), cols(0)]
        for n in range(2):
            wait(chunk, own_send.at[n, k])
            wait(half, fwd_send.at[n, k])
        for n in range(4):
            wait(chunk, core_send.at[n, k])

    for e in range(NP // 2):
        wait(scales.at[0, pl.ds(0, NG - 1)], sc_send.at[e])

    wait(stats.at[pl.ds(0, NT - 1)], st_recv)
    token = lax.broadcasted_iota(jnp.int32, (8, QB), 0) * QB + lax.broadcasted_iota(jnp.int32, (8, QB), 1)
    gap = jnp.sum(stats[:, 1], axis=0) - combine(stats[:, 0])
    logprob[...] = jnp.where(token < counts[0], gap, 0.0)
    wait(stats.at[pl.ds(0, NT - 1)], st_send)


def write(held, held_logprob, held_scale, quant, logprob, scale, sem):
    copies = [
        pltpu.make_async_copy(held.at[pl.ds(QB * i, QB)], quant.at[pl.ds(QB * i, QB)], sem.at[i]) for i in range(8)
    ]
    copies.append(pltpu.make_async_copy(held_logprob, logprob, sem.at[8]))
    copies.append(pltpu.make_async_copy(held_scale, scale, sem.at[9]))
    for copy in copies:
        copy.start()
    for copy in copies:
        copy.wait()


def local(panel, hidden, targets, counts):
    dma = pltpu.SemaphoreType.DMA
    vmem = pl.BlockSpec(memory_space=pltpu.VMEM)
    hbm = pl.BlockSpec(memory_space=pltpu.HBM)
    held = pl.pallas_call(
        kernel,
        out_shape=(
            pltpu.VMEM((8, QB), jnp.float32),
            pltpu.VMEM((ROWS, D), jnp.bfloat16),
            pltpu.VMEM((NG, NP * BLOCKS), jnp.bfloat16),
        ),
        in_specs=[hbm, hbm, hbm, pl.BlockSpec(memory_space=pltpu.SMEM)],
        out_specs=(vmem, vmem, vmem),
        scratch_shapes=[
            pltpu.VMEM((D, QB), jnp.bfloat16),
            pltpu.VMEM((ROWS, D), jnp.bfloat16),
            pltpu.VMEM((NP // 2, NG, 1, QB), jnp.float32),
            pltpu.VMEM((ROWS, ROWS), jnp.float32),
            pltpu.VMEM((8, QB), jnp.int32),
            pltpu.VMEM((NZ, 2, 8, QB), jnp.float32),
            pltpu.VMEM((NT, 2, 8, QB), jnp.float32),
            dma((NT,)), dma((NT,)), dma(()), dma(()), dma(()), dma(()),
            dma((2, NP)), dma((2, NP)), dma((4, NP)), dma((NP // 2,)), dma(()),
            dma((NP,)), dma((NP,)), dma((NP,)), dma((NP,)), dma((4, NP)), dma((NP // 2,)), dma(()),
        ],
        compiler_params=pltpu.CompilerParams(
            collective_id=0, has_side_effects=True, vmem_limit_bytes=VMEM_LIMIT
        ),
        cost_estimate=pl.CostEstimate(
            flops=2 * ROWS * ROWS * D, bytes_accessed=4 * ROWS * D, transcendentals=ROWS * ROWS
        ),
        name="refresh",
    )(
        pltpu.with_memory_space_constraint(panel.T, pltpu.HBM),
        hidden,
        pltpu.with_memory_space_constraint(targets.reshape(8, QB), pltpu.HBM),
        counts,
    )
    quant, logprob, scale = pl.pallas_call(
        write,
        out_shape=(
            pltpu.HBM((ROWS, D), jnp.bfloat16),
            pltpu.HBM((8, QB), jnp.float32),
            pltpu.HBM((NG, NP * BLOCKS), jnp.bfloat16),
        ),
        in_specs=[vmem] * 3,
        out_specs=(hbm,) * 3,
        scratch_shapes=[dma((10,))],
        compiler_params=pltpu.CompilerParams(vmem_limit_bytes=2 << 20),
        cost_estimate=pl.CostEstimate(flops=0, bytes_accessed=4 * ROWS * D, transcendentals=0),
        name="write",
    )(held[1], held[0], held[2])
    return logprob.reshape(ROWS), quant, scale


def solution(mesh):
    in_specs = (P("group", "tensor"), P("group", None), P("group"), P("group"))
    out_specs = (P("group"), P("tensor", None), P("tensor", None))
    return jax.shard_map(local, mesh=mesh, in_specs=in_specs, out_specs=out_specs, check_vma=False)
```

```python
import functools

import jax
import jax.numpy as jnp
from jax import lax
from jax.experimental import pallas as pl
from jax.experimental.pallas import tpu as pltpu
from jax.sharding import PartitionSpec as P

MESH = pl.DeviceIdType.MESH
QB = 128
NZ = 4
NG = 8
NT = 16
NP = 8
ROWS = 1024
D = 7168
SRC = D // NT
CW = 2 * SRC
BLOCKS = CW // QB
HALF = QB // 2
LEAD = 2
AHEAD = 4
LAG = 2
VMEM_LIMIT = 32 << 20


def kernel(
    panel, hidden, targets, counts,
    logprob, quant, scale,
    arrived, states, scales, logits, wanted, parts, stats,
    a2a_send, a2a_recv, hid_sem, tgt_sem, near_recv, near_send,
    own_send, fwd_send, core_send, sc_send, st_send, early_recv,
    prev_recv, next_recv, top_recv, bot_recv, core_recv, sc_recv, st_recv,
):
    g = lax.axis_index("group")
    t = lax.axis_index("tensor")
    z, c = g // 2, lax.rem(g, 2)
    gp = lax.rem(z + 3, NZ) * 2 + c
    gn = lax.rem(z + 1, NZ) * 2 + c
    gf = lax.rem(z + 2, NZ) * 2 + c
    go = z * 2 + 1 - c
    y, xh, odd = t // 4, lax.rem(t, 4) // 2, lax.rem(t, 2)

    def shift(k):
        def among(*steps):
            return functools.reduce(jnp.logical_or, [k == n for n in steps])

        dy = jnp.where(among(1, 4), 1, jnp.where(among(3, 5), 3, jnp.where(k >= 6, 2, 0)))
        return dy, jnp.where(among(2, 4, 5, 7), 1, 0)

    def pair(k):
        dy, dx = shift(k)
        return lax.rem(y + dy, 4) * 2 + lax.rem(xh + dx, 2)

    def cols(p):
        return pl.ds(pl.multiple_of(p * CW, CW), CW)

    def rows(b, first=0, size=QB):
        return pl.ds(pl.multiple_of(b * QB + first, HALF), size)

    def tens(u):
        return pl.ds(pl.multiple_of(u * QB, QB), QB)

    def block_of(u):
        return pl.ds(pl.multiple_of(u * SRC, SRC), SRC)

    def wait(ref, sem):
        pltpu.make_async_copy(ref, ref, sem).wait()

    def remote(src, dst, send, recv, to):
        pltpu.make_async_remote_copy(
            src_ref=src, dst_ref=dst, send_sem=send, recv_sem=recv, device_id=to, device_id_type=MESH
        ).start()

    pltpu.make_async_copy(panel.at[:, tens(t)], arrived.at[block_of(t)], a2a_recv.at[t]).start()
    barrier = pltpu.get_barrier_semaphore()
    p0 = pair(0)

    @pl.loop(1, NT)
    def _(s):
        pl.semaphore_signal(barrier, inc=1, device_id=(g, lax.rem(t + s, NT)), device_id_type=MESH)

    @pl.loop(1, NG)
    def _(s):
        pl.semaphore_signal(barrier, inc=1, device_id=(lax.rem(g + s, NG), t), device_id_type=MESH)

    pltpu.make_async_copy(targets, wanted, tgt_sem).start()

    def batch(k):
        return k // 2

    def quantize(k, first, count):
        p, e = pair(k), batch(k)
        lane = lax.broadcasted_iota(jnp.int32, (1, QB), 1)
        tile = scales[e, g]
        for i in range(count):
            at = pl.multiple_of(p * CW + (first + i) * QB, QB)
            block = arrived[pl.ds(at, QB)].astype(jnp.float32)
            largest = jnp.max(jnp.abs(block), axis=(0, 1), keepdims=True)
            s = ((largest + 1e-06) / 448.0).astype(jnp.bfloat16).astype(jnp.float32)
            quant[rows(g), pl.ds(at, QB)] = (block / s).astype(jnp.bfloat16).T
            tile = jnp.where(lane == p * BLOCKS + first + i, jnp.broadcast_to(s, (1, QB)), tile)
        scales[e, g] = tile

    def send_own(k, at, width, early=False):
        block = quant.at[rows(g), pl.ds(pl.multiple_of(at, QB), width)]
        remote(block, block, own_send.at[0, k], early_recv.at[0] if early else prev_recv.at[k], (gn, t))
        remote(block, block, own_send.at[1, k], early_recv.at[1] if early else next_recv.at[k], (gp, t))
        remote(block, block, core_send.at[0, k], core_recv.at[0, k], (go, t))

    def send_scales(e):
        @pl.loop(1, NG)
        def _(s):
            remote(scales.at[e, g], scales.at[e, g], sc_send.at[e], sc_recv.at[e], (lax.rem(g + s, NG), t))

    pl.semaphore_wait(barrier, NT - 1 + NG - 1)

    def send_block(u):
        remote(panel.at[:, tens(u)], arrived.at[block_of(t)], a2a_send.at[u], a2a_recv.at[t], (g, u))

    def send_pair(j):
        dy, dx = shift(j)
        q = lax.rem(y + 4 - dy, 4) * 2 + lax.rem(xh + dx, 2)
        send_block(2 * q)
        send_block(2 * q + 1)

    other = 2 * p0 + 1 - odd
    edge = HALF + QB

    def columns(u, at, size):
        return pl.ds(pl.multiple_of(u * SRC + at, HALF), size)

    def near_part(u, side, first):
        at = (SRC - edge) * (1 - side) if first else edge * side
        return at, (edge if first else SRC - edge)

    for part in (True, False):
        at, size = near_part(t, odd, part)
        remote(
            panel.at[pl.ds(pl.multiple_of(at, HALF), size), tens(other)],
            arrived.at[columns(t, at, size)],
            near_send if part else a2a_send.at[other],
            near_recv if part else a2a_recv.at[t],
            (g, other),
        )

    for e in range(NP // 2):
        scales[e, g] = jnp.zeros((1, QB), jnp.float32)
    wait(arrived.at[block_of(t)], a2a_recv.at[t])
    quantize(0, 4 * odd, 3)
    send_own(0, p0 * CW + 4 * odd * QB, 3 * QB, early=True)
    for j in range(1, AHEAD):
        send_pair(j)
    pltpu.make_async_copy(hidden, states, hid_sem).start()
    logits[...] = jnp.zeros_like(logits)

    def forward(k, at):
        wait(quant.at[rows(gp), at], early_recv.at[0] if k is None else prev_recv.at[k])
        k0 = 0 if k is None else k
        top = quant.at[rows(gp, 0, HALF), at]
        remote(top, top, fwd_send.at[0, k0], top_recv.at[k0], (gn, t))
        wait(quant.at[rows(gn), at], early_recv.at[1] if k is None else next_recv.at[k])
        bot = quant.at[rows(gn, HALF, HALF), at]
        remote(bot, bot, fwd_send.at[1, k0], bot_recv.at[k0], (gp, t))

    def step_near(k):
        p = pair(k)

        @pl.when(k == 0)
        def _():
            forward(k, pl.ds(pl.multiple_of(p * CW + (3 - 3 * odd) * QB, QB), 4 * QB))

        @pl.when(k > 0)
        def _():
            forward(k, cols(p))

        for n, b in ((1, gp), (2, gn)):
            block = quant.at[rows(b), cols(p)]
            remote(block, block, core_send.at[n, k], core_recv.at[n, k], (go, t))

    for part in (True, False):
        at, size = near_part(other, 1 - odd, part)
        wait(arrived.at[columns(other, at, size)], near_recv if part else a2a_recv.at[other])
        first = (3 - 1 * odd) if part else (5 - 5 * odd)
        quantize(0, first, 2)
        send_own(0, p0 * CW + first * QB, 2 * QB)

    forward(None, pl.ds(pl.multiple_of(p0 * CW + 4 * odd * QB, QB), 3 * QB))

    def step_own(k):
        p = pair(k)
        wait(arrived.at[block_of(2 * p)], a2a_recv.at[2 * p])
        wait(arrived.at[block_of(2 * p + 1)], a2a_recv.at[2 * p + 1])
        quantize(k, 0, BLOCKS)

        @pl.when(lax.rem(k, 2) == 1)
        def _():
            send_scales(batch(k))

        send_own(k, p * CW, CW)

    def step_far(k):
        p = pair(k)
        wait(quant.at[rows(gf, 0, HALF), cols(p)], top_recv.at[k])
        wait(quant.at[rows(gf, HALF, HALF), cols(p)], bot_recv.at[k])
        block = quant.at[rows(gf), cols(p)]
        remote(block, block, core_send.at[3, k], core_recv.at[3, k], (go, t))

    def dot(k, b):
        p = pair(k)
        both = []
        for h in range(2):
            s = pltpu.roll(scales[batch(k), 2 * b + h], lax.rem(QB - p * BLOCKS, QB), 1)
            spread = jnp.concatenate([jnp.broadcast_to(s[0:1, i:i + 1], (1, QB)) for i in range(BLOCKS)], axis=1)
            q = quant[rows(2 * b + h), cols(p)].astype(jnp.float32)
            both.append((q * spread).astype(jnp.bfloat16))
        w = jnp.concatenate(both, axis=0)
        at = pl.ds(pl.multiple_of(b * 256, 256), 256)
        logits[at, :] += lax.dot_general(
            w, states[:, cols(p)], (((1,), (1,)), ((), ())), preferred_element_type=jnp.float32
        )

    def dot_own(k):
        wait(quant.at[rows(0), cols(0)], core_recv.at[0, k])
        dot(k, z)

    def dot_near(k):
        for n in range(1, 3):
            wait(quant.at[rows(0), cols(0)], core_recv.at[n, k])

        @pl.loop(0, 2)
        def _(j):
            dot(k, lax.rem(z + 1 + 2 * j, NZ))

    def dot_far(k):
        wait(quant.at[rows(0), cols(0)], core_recv.at[3, k])
        dot(k, lax.rem(z + 2, NZ))

    p1 = pair(1)
    for first, count in ((0, 3), (3, 4)):
        source = 2 * p1 + first // 3
        wait(arrived.at[block_of(source)], a2a_recv.at[source])
        quantize(1, first, count)
        if first:
            send_scales(0)
        send_own(1, p1 * CW + first * QB, count * QB)
    send_pair(AHEAD)
    for k in range(2, LEAD):
        send_pair(AHEAD - 1 + k)
        step_own(jnp.int32(k))

    @pl.loop(0, NP)
    def _(k):
        @pl.when(k < NP - (AHEAD - 1 + LEAD))
        def _():
            send_pair(k + AHEAD - 1 + LEAD)

        @pl.when(k < NP - LEAD)
        def _():
            step_own(k + LEAD)

        @pl.when(lax.rem(k, 2) == 1)
        def _():
            dot_own(k)

        step_near(k)

        @pl.when(k >= LAG)
        def _():
            step_far(k - LAG)

        @pl.when(k == 0)
        def _():
            pltpu.make_async_copy(hidden, states, hid_sem).wait()

        @pl.when(lax.rem(k, 2) == 0)
        def _():
            wait(scales.at[0, pl.ds(0, NG - 1)], sc_recv.at[batch(k)])
            dot_own(k)

        dot_near(k)

        @pl.when(k >= LAG)
        def _():
            dot_far(k - LAG)

    row = lax.broadcasted_iota(jnp.int32, (256, QB), 0)
    pltpu.make_async_copy(targets, wanted, tgt_sem).wait()

    def measure(b):
        @pl.loop(0, 8, unroll=4)
        def _(j):
            x = logits[pl.ds(pl.multiple_of(b * 256, 256), 256), pl.ds(pl.multiple_of(j * QB, QB), QB)]
            v = wanted[pl.ds(j, 1), :]
            mine = lax.rem(v // QB, NT) == t
            column = jnp.where(mine, v // (NT * QB) * QB + lax.rem(v, QB) - b * 256, -1)
            top = jnp.max(x, axis=0, keepdims=True)
            total = jnp.sum(jnp.exp(x - top), axis=0, keepdims=True)
            parts[b, 0, pl.ds(j, 1), :] = top + jnp.log(total)
            parts[b, 1, pl.ds(j, 1), :] = jnp.sum(jnp.where(row == column, x, 0.0), axis=0, keepdims=True)

    def combine(lses):
        top = jnp.max(lses, axis=0)
        return top + jnp.log(jnp.sum(jnp.exp(lses - top[None]), axis=0))

    for k in range(NP - LAG, NP - 2):
        step_far(k)
        dot_far(k)

    step_far(NP - 2)

    @pl.loop(0, 3)
    def _(j):
        measure(lax.rem(z + 3 + j, NZ))

    step_far(NP - 1)
    dot_far(NP - 2)
    dot_far(NP - 1)
    measure(lax.rem(z + 2, NZ))
    stats[t, 0] = combine(parts[:, 0])
    stats[t, 1] = jnp.sum(parts[:, 1], axis=0)

    @pl.loop(1, NT)
    def _(s):
        remote(stats.at[t], stats.at[t], st_send, st_recv, (g, lax.rem(t + s, NT)))

    table = jnp.concatenate([jnp.sum(scales[:, b], axis=0) for b in range(NG)], axis=0)
    scale[...] = table[:, :NP * BLOCKS].astype(jnp.bfloat16)

    wait(panel.at[pl.ds(0, edge), tens(0)], near_send)
    wait(panel.at[pl.ds(0, SRC - edge), tens(0)], a2a_send.at[other])

    @pl.loop(1, NP)
    def _(j):
        q = lax.rem(p0 + j, NP)
        wait(panel.at[:, tens(0)], a2a_send.at[2 * q])
        wait(panel.at[:, tens(0)], a2a_send.at[2 * q + 1])

    @pl.loop(0, NP)
    def _(k):
        chunk = quant.at[rows(0), cols(0)]
        half = quant.at[rows(0, 0, HALF), cols(0)]
        for n in range(2):
            wait(chunk, own_send.at[n, k])
            wait(half, fwd_send.at[n, k])
        for n in range(4):
            wait(chunk, core_send.at[n, k])

    for e in range(NP // 2):
        wait(scales.at[0, pl.ds(0, NG - 1)], sc_send.at[e])

    wait(stats.at[pl.ds(0, NT - 1)], st_recv)
    token = lax.broadcasted_iota(jnp.int32, (8, QB), 0) * QB + lax.broadcasted_iota(jnp.int32, (8, QB), 1)
    gap = jnp.sum(stats[:, 1], axis=0) - combine(stats[:, 0])
    logprob[...] = jnp.where(token < counts[0], gap, 0.0)
    wait(stats.at[pl.ds(0, NT - 1)], st_send)


def write(held, held_logprob, held_scale, quant, logprob, scale, sem):
    copies = [
        pltpu.make_async_copy(held.at[pl.ds(QB * i, QB)], quant.at[pl.ds(QB * i, QB)], sem.at[i]) for i in range(8)
    ]
    copies.append(pltpu.make_async_copy(held_logprob, logprob, sem.at[8]))
    copies.append(pltpu.make_async_copy(held_scale, scale, sem.at[9]))
    for copy in copies:
        copy.start()
    for copy in copies:
        copy.wait()


def local(panel, hidden, targets, counts):
    dma = pltpu.SemaphoreType.DMA
    vmem = pl.BlockSpec(memory_space=pltpu.VMEM)
    hbm = pl.BlockSpec(memory_space=pltpu.HBM)
    held = pl.pallas_call(
        kernel,
        out_shape=(
            pltpu.VMEM((8, QB), jnp.float32),
            pltpu.VMEM((ROWS, D), jnp.bfloat16),
            pltpu.VMEM((NG, NP * BLOCKS), jnp.bfloat16),
        ),
        in_specs=[hbm, hbm, hbm, pl.BlockSpec(memory_space=pltpu.SMEM)],
        out_specs=(vmem, vmem, vmem),
        scratch_shapes=[
            pltpu.VMEM((D, QB), jnp.bfloat16),
            pltpu.VMEM((ROWS, D), jnp.bfloat16),
            pltpu.VMEM((NP // 2, NG, 1, QB), jnp.float32),
            pltpu.VMEM((ROWS, ROWS), jnp.float32),
            pltpu.VMEM((8, QB), jnp.int32),
            pltpu.VMEM((NZ, 2, 8, QB), jnp.float32),
            pltpu.VMEM((NT, 2, 8, QB), jnp.float32),
            dma((NT,)), dma((NT,)), dma(()), dma(()), dma(()), dma(()),
            dma((2, NP)), dma((2, NP)), dma((4, NP)), dma((NP // 2,)), dma(()), dma((2,)),
            dma((NP,)), dma((NP,)), dma((NP,)), dma((NP,)), dma((4, NP)), dma((NP // 2,)), dma(()),
        ],
        compiler_params=pltpu.CompilerParams(
            collective_id=0, has_side_effects=True, vmem_limit_bytes=VMEM_LIMIT
        ),
        cost_estimate=pl.CostEstimate(
            flops=2 * ROWS * ROWS * D, bytes_accessed=4 * ROWS * D, transcendentals=ROWS * ROWS
        ),
        name="refresh",
    )(
        pltpu.with_memory_space_constraint(panel.T, pltpu.HBM),
        hidden,
        pltpu.with_memory_space_constraint(targets.reshape(8, QB), pltpu.HBM),
        counts,
    )
    quant, logprob, scale = pl.pallas_call(
        write,
        out_shape=(
            pltpu.HBM((ROWS, D), jnp.bfloat16),
            pltpu.HBM((8, QB), jnp.float32),
            pltpu.HBM((NG, NP * BLOCKS), jnp.bfloat16),
        ),
        in_specs=[vmem] * 3,
        out_specs=(hbm,) * 3,
        scratch_shapes=[dma((10,))],
        compiler_params=pltpu.CompilerParams(vmem_limit_bytes=2 << 20),
        cost_estimate=pl.CostEstimate(flops=0, bytes_accessed=4 * ROWS * D, transcendentals=0),
        name="write",
    )(held[1], held[0], held[2])
    return logprob.reshape(ROWS), quant, scale


def solution(mesh):
    in_specs = (P("group", "tensor"), P("group", None), P("group"), P("group"))
    out_specs = (P("group"), P("tensor", None), P("tensor", None))
    return jax.shard_map(local, mesh=mesh, in_specs=in_specs, out_specs=out_specs, check_vma=False)
```

```python
import functools

import jax
import jax.numpy as jnp
from jax import lax
from jax.experimental import pallas as pl
from jax.experimental.pallas import tpu as pltpu
from jax.sharding import PartitionSpec as P

MESH = pl.DeviceIdType.MESH
QB = 128
NZ = 4
NG = 8
NT = 16
NP = 8
ROWS = 1024
D = 7168
SRC = D // NT
CW = 2 * SRC
BLOCKS = CW // QB
HALF = QB // 2
LEAD = 3
AHEAD = 4
LAG = 3
VMEM_LIMIT = 32 << 20


def kernel(
    panel, hidden, targets, counts,
    logprob, quant, scale,
    arrived, states, scales, logits, wanted, parts, stats,
    a2a_send, a2a_recv, hid_sem, tgt_sem, near_recv, near_send,
    own_send, fwd_send, core_send, sc_send, st_send, early_recv,
    prev_recv, next_recv, top_recv, bot_recv, core_recv, sc_recv, st_recv,
):
    g = lax.axis_index("group")
    t = lax.axis_index("tensor")
    z, c = g // 2, lax.rem(g, 2)
    gp = lax.rem(z + 3, NZ) * 2 + c
    gn = lax.rem(z + 1, NZ) * 2 + c
    gf = lax.rem(z + 2, NZ) * 2 + c
    go = z * 2 + 1 - c
    y, xh, odd = t // 4, lax.rem(t, 4) // 2, lax.rem(t, 2)

    def shift(k):
        def among(*steps):
            return functools.reduce(jnp.logical_or, [k == n for n in steps])

        dy = jnp.where(among(1, 4), 1, jnp.where(among(3, 5), 3, jnp.where(k >= 6, 2, 0)))
        return dy, jnp.where(among(2, 4, 5, 7), 1, 0)

    def pair(k):
        dy, dx = shift(k)
        return lax.rem(y + dy, 4) * 2 + lax.rem(xh + dx, 2)

    def cols(p):
        return pl.ds(pl.multiple_of(p * CW, CW), CW)

    def rows(b, first=0, size=QB):
        return pl.ds(pl.multiple_of(b * QB + first, HALF), size)

    def tens(u):
        return pl.ds(pl.multiple_of(u * QB, QB), QB)

    def block_of(u):
        return pl.ds(pl.multiple_of(u * SRC, SRC), SRC)

    def wait(ref, sem):
        pltpu.make_async_copy(ref, ref, sem).wait()

    def remote(src, dst, send, recv, to):
        pltpu.make_async_remote_copy(
            src_ref=src, dst_ref=dst, send_sem=send, recv_sem=recv, device_id=to, device_id_type=MESH
        ).start()

    pltpu.make_async_copy(panel.at[:, tens(t)], arrived.at[block_of(t)], a2a_recv.at[t]).start()
    barrier = pltpu.get_barrier_semaphore()
    p0 = pair(0)

    @pl.loop(1, NT)
    def _(s):
        pl.semaphore_signal(barrier, inc=1, device_id=(g, lax.rem(t + s, NT)), device_id_type=MESH)

    @pl.loop(1, NG)
    def _(s):
        pl.semaphore_signal(barrier, inc=1, device_id=(lax.rem(g + s, NG), t), device_id_type=MESH)

    pltpu.make_async_copy(targets, wanted, tgt_sem).start()

    def batch(k):
        return k // 2

    def quantize(k, first, count):
        p, e = pair(k), batch(k)
        lane = lax.broadcasted_iota(jnp.int32, (1, QB), 1)
        tile = scales[e, g]
        for i in range(count):
            at = pl.multiple_of(p * CW + (first + i) * QB, QB)
            block = arrived[pl.ds(at, QB)].astype(jnp.float32)
            largest = jnp.max(jnp.abs(block), axis=(0, 1), keepdims=True)
            s = ((largest + 1e-06) / 448.0).astype(jnp.bfloat16).astype(jnp.float32)
            quant[rows(g), pl.ds(at, QB)] = (block / s).astype(jnp.bfloat16).T
            tile = jnp.where(lane == p * BLOCKS + first + i, jnp.broadcast_to(s, (1, QB)), tile)
        scales[e, g] = tile

    def send_own(k, at, width, early=False):
        block = quant.at[rows(g), pl.ds(pl.multiple_of(at, QB), width)]
        remote(block, block, own_send.at[0, k], early_recv.at[0] if early else prev_recv.at[k], (gn, t))
        remote(block, block, own_send.at[1, k], early_recv.at[1] if early else next_recv.at[k], (gp, t))
        remote(block, block, core_send.at[0, k], core_recv.at[0, k], (go, t))

    def send_scales(e):
        @pl.loop(1, NG)
        def _(s):
            remote(scales.at[e, g], scales.at[e, g], sc_send.at[e], sc_recv.at[e], (lax.rem(g + s, NG), t))

    pl.semaphore_wait(barrier, NT - 1 + NG - 1)

    def send_block(u):
        remote(panel.at[:, tens(u)], arrived.at[block_of(t)], a2a_send.at[u], a2a_recv.at[t], (g, u))

    def send_pair(j):
        dy, dx = shift(j)
        q = lax.rem(y + 4 - dy, 4) * 2 + lax.rem(xh + dx, 2)
        send_block(2 * q)
        send_block(2 * q + 1)

    other = 2 * p0 + 1 - odd
    edge = HALF + QB

    def columns(u, at, size):
        return pl.ds(pl.multiple_of(u * SRC + at, HALF), size)

    def near_part(u, side, first):
        at = (SRC - edge) * (1 - side) if first else edge * side
        return at, (edge if first else SRC - edge)

    for part in (True, False):
        at, size = near_part(t, odd, part)
        remote(
            panel.at[pl.ds(pl.multiple_of(at, HALF), size), tens(other)],
            arrived.at[columns(t, at, size)],
            near_send if part else a2a_send.at[other],
            near_recv if part else a2a_recv.at[t],
            (g, other),
        )

    for e in range(NP // 2):
        scales[e, g] = jnp.zeros((1, QB), jnp.float32)
    wait(arrived.at[block_of(t)], a2a_recv.at[t])
    quantize(0, 4 * odd, 3)
    send_own(0, p0 * CW + 4 * odd * QB, 3 * QB, early=True)
    for j in range(1, AHEAD):
        send_pair(j)
    pltpu.make_async_copy(hidden, states, hid_sem).start()
    logits[...] = jnp.zeros_like(logits)

    def forward(k, at):
        wait(quant.at[rows(gp), at], early_recv.at[0] if k is None else prev_recv.at[k])
        k0 = 0 if k is None else k
        top = quant.at[rows(gp, 0, HALF), at]
        remote(top, top, fwd_send.at[0, k0], top_recv.at[k0], (gn, t))
        wait(quant.at[rows(gn), at], early_recv.at[1] if k is None else next_recv.at[k])
        bot = quant.at[rows(gn, HALF, HALF), at]
        remote(bot, bot, fwd_send.at[1, k0], bot_recv.at[k0], (gp, t))

    def step_near(k):
        p = pair(k)

        @pl.when(k == 0)
        def _():
            forward(k, pl.ds(pl.multiple_of(p * CW + (3 - 3 * odd) * QB, QB), 4 * QB))

        @pl.when(k > 0)
        def _():
            forward(k, cols(p))

        for n, b in ((1, gp), (2, gn)):
            block = quant.at[rows(b), cols(p)]
            remote(block, block, core_send.at[n, k], core_recv.at[n, k], (go, t))

    for part in (True, False):
        at, size = near_part(other, 1 - odd, part)
        wait(arrived.at[columns(other, at, size)], near_recv if part else a2a_recv.at[other])
        first = (3 - 1 * odd) if part else (5 - 5 * odd)
        quantize(0, first, 2)
        send_own(0, p0 * CW + first * QB, 2 * QB)

    forward(None, pl.ds(pl.multiple_of(p0 * CW + 4 * odd * QB, QB), 3 * QB))

    def step_own(k):
        p = pair(k)
        wait(arrived.at[block_of(2 * p)], a2a_recv.at[2 * p])
        wait(arrived.at[block_of(2 * p + 1)], a2a_recv.at[2 * p + 1])
        quantize(k, 0, BLOCKS)

        @pl.when(lax.rem(k, 2) == 1)
        def _():
            send_scales(batch(k))

        send_own(k, p * CW, CW)

    def step_far(k):
        p = pair(k)
        wait(quant.at[rows(gf, 0, HALF), cols(p)], top_recv.at[k])
        wait(quant.at[rows(gf, HALF, HALF), cols(p)], bot_recv.at[k])
        block = quant.at[rows(gf), cols(p)]
        remote(block, block, core_send.at[3, k], core_recv.at[3, k], (go, t))

    def dot(k, b):
        p = pair(k)
        both = []
        for h in range(2):
            s = pltpu.roll(scales[batch(k), 2 * b + h], lax.rem(QB - p * BLOCKS, QB), 1)
            spread = jnp.concatenate([jnp.broadcast_to(s[0:1, i:i + 1], (1, QB)) for i in range(BLOCKS)], axis=1)
            q = quant[rows(2 * b + h), cols(p)].astype(jnp.float32)
            both.append((q * spread).astype(jnp.bfloat16))
        w = jnp.concatenate(both, axis=0)
        at = pl.ds(pl.multiple_of(b * 256, 256), 256)
        logits[at, :] += lax.dot_general(
            w, states[:, cols(p)], (((1,), (1,)), ((), ())), preferred_element_type=jnp.float32
        )

    def dot_own(k):
        wait(quant.at[rows(0), cols(0)], core_recv.at[0, k])
        dot(k, z)

    def dot_near(k):
        for n in range(1, 3):
            wait(quant.at[rows(0), cols(0)], core_recv.at[n, k])

        @pl.loop(0, 2)
        def _(j):
            dot(k, lax.rem(z + 1 + 2 * j, NZ))

    def dot_far(k):
        wait(quant.at[rows(0), cols(0)], core_recv.at[3, k])
        dot(k, lax.rem(z + 2, NZ))

    p1 = pair(1)
    for first, count in ((0, 3), (3, 4)):
        source = 2 * p1 + first // 3
        wait(arrived.at[block_of(source)], a2a_recv.at[source])
        quantize(1, first, count)
        if first:
            send_scales(0)
        send_own(1, p1 * CW + first * QB, count * QB)
    send_pair(AHEAD)
    for k in range(2, LEAD):
        send_pair(AHEAD - 1 + k)
        step_own(jnp.int32(k))

    @pl.loop(0, NP)
    def _(k):
        @pl.when(k < NP - (AHEAD - 1 + LEAD))
        def _():
            send_pair(k + AHEAD - 1 + LEAD)

        @pl.when(k < NP - LEAD)
        def _():
            step_own(k + LEAD)

        @pl.when(lax.rem(k, 2) == 1)
        def _():
            dot_own(k)

        step_near(k)

        @pl.when(k >= LAG)
        def _():
            step_far(k - LAG)

        @pl.when(k == 0)
        def _():
            pltpu.make_async_copy(hidden, states, hid_sem).wait()

        @pl.when(lax.rem(k, 2) == 0)
        def _():
            wait(scales.at[0, pl.ds(0, NG - 1)], sc_recv.at[batch(k)])
            dot_own(k)

        dot_near(k)

        @pl.when(k >= LAG)
        def _():
            dot_far(k - LAG)

    row = lax.broadcasted_iota(jnp.int32, (256, QB), 0)
    pltpu.make_async_copy(targets, wanted, tgt_sem).wait()

    def measure(b):
        @pl.loop(0, 8, unroll=4)
        def _(j):
            x = logits[pl.ds(pl.multiple_of(b * 256, 256), 256), pl.ds(pl.multiple_of(j * QB, QB), QB)]
            v = wanted[pl.ds(j, 1), :]
            mine = lax.rem(v // QB, NT) == t
            column = jnp.where(mine, v // (NT * QB) * QB + lax.rem(v, QB) - b * 256, -1)
            top = jnp.max(x, axis=0, keepdims=True)
            total = jnp.sum(jnp.exp(x - top), axis=0, keepdims=True)
            parts[b, 0, pl.ds(j, 1), :] = top + jnp.log(total)
            parts[b, 1, pl.ds(j, 1), :] = jnp.sum(jnp.where(row == column, x, 0.0), axis=0, keepdims=True)

    def combine(lses):
        top = jnp.max(lses, axis=0)
        return top + jnp.log(jnp.sum(jnp.exp(lses - top[None]), axis=0))

    for k in range(NP - LAG, NP - 2):
        step_far(k)
        dot_far(k)

    step_far(NP - 2)

    @pl.loop(0, 3)
    def _(j):
        measure(lax.rem(z + 3 + j, NZ))

    step_far(NP - 1)
    dot_far(NP - 2)
    dot_far(NP - 1)
    measure(lax.rem(z + 2, NZ))
    stats[t, 0] = combine(parts[:, 0])
    stats[t, 1] = jnp.sum(parts[:, 1], axis=0)

    @pl.loop(1, NT)
    def _(s):
        remote(stats.at[t], stats.at[t], st_send, st_recv, (g, lax.rem(t + s, NT)))

    table = jnp.concatenate([jnp.sum(scales[:, b], axis=0) for b in range(NG)], axis=0)
    scale[...] = table[:, :NP * BLOCKS].astype(jnp.bfloat16)

    wait(panel.at[pl.ds(0, edge), tens(0)], near_send)
    wait(panel.at[pl.ds(0, SRC - edge), tens(0)], a2a_send.at[other])

    @pl.loop(1, NP)
    def _(j):
        q = lax.rem(p0 + j, NP)
        wait(panel.at[:, tens(0)], a2a_send.at[2 * q])
        wait(panel.at[:, tens(0)], a2a_send.at[2 * q + 1])

    @pl.loop(0, NP)
    def _(k):
        chunk = quant.at[rows(0), cols(0)]
        half = quant.at[rows(0, 0, HALF), cols(0)]
        for n in range(2):
            wait(chunk, own_send.at[n, k])
            wait(half, fwd_send.at[n, k])
        for n in range(4):
            wait(chunk, core_send.at[n, k])

    for e in range(NP // 2):
        wait(scales.at[0, pl.ds(0, NG - 1)], sc_send.at[e])

    wait(stats.at[pl.ds(0, NT - 1)], st_recv)
    token = lax.broadcasted_iota(jnp.int32, (8, QB), 0) * QB + lax.broadcasted_iota(jnp.int32, (8, QB), 1)
    gap = jnp.sum(stats[:, 1], axis=0) - combine(stats[:, 0])
    logprob[...] = jnp.where(token < counts[0], gap, 0.0)
    wait(stats.at[pl.ds(0, NT - 1)], st_send)


def write(held, held_logprob, held_scale, quant, logprob, scale, sem):
    copies = [
        pltpu.make_async_copy(held.at[pl.ds(QB * i, QB)], quant.at[pl.ds(QB * i, QB)], sem.at[i]) for i in range(8)
    ]
    copies.append(pltpu.make_async_copy(held_logprob, logprob, sem.at[8]))
    copies.append(pltpu.make_async_copy(held_scale, scale, sem.at[9]))
    for copy in copies:
        copy.start()
    for copy in copies:
        copy.wait()


def local(panel, hidden, targets, counts):
    dma = pltpu.SemaphoreType.DMA
    vmem = pl.BlockSpec(memory_space=pltpu.VMEM)
    hbm = pl.BlockSpec(memory_space=pltpu.HBM)
    held = pl.pallas_call(
        kernel,
        out_shape=(
            pltpu.VMEM((8, QB), jnp.float32),
            pltpu.VMEM((ROWS, D), jnp.bfloat16),
            pltpu.VMEM((NG, NP * BLOCKS), jnp.bfloat16),
        ),
        in_specs=[hbm, hbm, hbm, pl.BlockSpec(memory_space=pltpu.SMEM)],
        out_specs=(vmem, vmem, vmem),
        scratch_shapes=[
            pltpu.VMEM((D, QB), jnp.bfloat16),
            pltpu.VMEM((ROWS, D), jnp.bfloat16),
            pltpu.VMEM((NP // 2, NG, 1, QB), jnp.float32),
            pltpu.VMEM((ROWS, ROWS), jnp.float32),
            pltpu.VMEM((8, QB), jnp.int32),
            pltpu.VMEM((NZ, 2, 8, QB), jnp.float32),
            pltpu.VMEM((NT, 2, 8, QB), jnp.float32),
            dma((NT,)), dma((NT,)), dma(()), dma(()), dma(()), dma(()),
            dma((2, NP)), dma((2, NP)), dma((4, NP)), dma((NP // 2,)), dma(()), dma((2,)),
            dma((NP,)), dma((NP,)), dma((NP,)), dma((NP,)), dma((4, NP)), dma((NP // 2,)), dma(()),
        ],
        compiler_params=pltpu.CompilerParams(
            collective_id=0, has_side_effects=True, vmem_limit_bytes=VMEM_LIMIT
        ),
        cost_estimate=pl.CostEstimate(
            flops=2 * ROWS * ROWS * D, bytes_accessed=4 * ROWS * D, transcendentals=ROWS * ROWS
        ),
        name="refresh",
    )(
        pltpu.with_memory_space_constraint(panel.T, pltpu.HBM),
        hidden,
        pltpu.with_memory_space_constraint(targets.reshape(8, QB), pltpu.HBM),
        counts,
    )
    quant, logprob, scale = pl.pallas_call(
        write,
        out_shape=(
            pltpu.HBM((ROWS, D), jnp.bfloat16),
            pltpu.HBM((8, QB), jnp.float32),
            pltpu.HBM((NG, NP * BLOCKS), jnp.bfloat16),
        ),
        in_specs=[vmem] * 3,
        out_specs=(hbm,) * 3,
        scratch_shapes=[dma((10,))],
        compiler_params=pltpu.CompilerParams(vmem_limit_bytes=2 << 20),
        cost_estimate=pl.CostEstimate(flops=0, bytes_accessed=4 * ROWS * D, transcendentals=0),
        name="write",
    )(held[1], held[0], held[2])
    return logprob.reshape(ROWS), quant, scale


def solution(mesh):
    in_specs = (P("group", "tensor"), P("group", None), P("group"), P("group"))
    out_specs = (P("group"), P("tensor", None), P("tensor", None))
    return jax.shard_map(local, mesh=mesh, in_specs=in_specs, out_specs=out_specs, check_vma=False)
```

```python
import functools

import jax
import jax.numpy as jnp
from jax import lax
from jax.experimental import pallas as pl
from jax.experimental.pallas import tpu as pltpu
from jax.sharding import PartitionSpec as P

MESH = pl.DeviceIdType.MESH
QB = 128
NZ = 4
NG = 8
NT = 16
NP = 8
ROWS = 1024
D = 7168
SRC = D // NT
CW = 2 * SRC
BLOCKS = CW // QB
HALF = QB // 2
LEAD = 3
AHEAD = 4
LAG = 3
VMEM_LIMIT = 32 << 20


def kernel(
    panel, hidden, targets, counts,
    logprob, quant, scale,
    arrived, states, scales, logits, wanted, parts, stats,
    a2a_send, a2a_recv, hid_sem, tgt_sem, near_recv, near_send,
    own_send, fwd_send, core_send, sc_send, st_send, early_recv,
    prev_recv, next_recv, top_recv, bot_recv, core_recv, sc_recv, st_recv,
):
    g = lax.axis_index("group")
    t = lax.axis_index("tensor")
    z, c = g // 2, lax.rem(g, 2)
    gp = lax.rem(z + 3, NZ) * 2 + c
    gn = lax.rem(z + 1, NZ) * 2 + c
    gf = lax.rem(z + 2, NZ) * 2 + c
    go = z * 2 + 1 - c
    y, xh, odd = t // 4, lax.rem(t, 4) // 2, lax.rem(t, 2)

    def shift(k):
        def among(*steps):
            return functools.reduce(jnp.logical_or, [k == n for n in steps])

        dy = jnp.where(among(1, 4), 1, jnp.where(among(3, 5), 3, jnp.where(k >= 6, 2, 0)))
        return dy, jnp.where(among(2, 4, 5, 7), 1, 0)

    def pair(k):
        dy, dx = shift(k)
        return lax.rem(y + dy, 4) * 2 + lax.rem(xh + dx, 2)

    def cols(p):
        return pl.ds(pl.multiple_of(p * CW, CW), CW)

    def rows(b, first=0, size=QB):
        return pl.ds(pl.multiple_of(b * QB + first, HALF), size)

    def tens(u):
        return pl.ds(pl.multiple_of(u * QB, QB), QB)

    def block_of(u):
        return pl.ds(pl.multiple_of(u * SRC, SRC), SRC)

    def wait(ref, sem):
        pltpu.make_async_copy(ref, ref, sem).wait()

    def remote(src, dst, send, recv, to):
        pltpu.make_async_remote_copy(
            src_ref=src, dst_ref=dst, send_sem=send, recv_sem=recv, device_id=to, device_id_type=MESH
        ).start()

    pltpu.make_async_copy(panel.at[:, tens(t)], arrived.at[block_of(t)], a2a_recv.at[t]).start()
    barrier = pltpu.get_barrier_semaphore()
    p0 = pair(0)

    @pl.loop(1, NT)
    def _(s):
        pl.semaphore_signal(barrier, inc=1, device_id=(g, lax.rem(t + s, NT)), device_id_type=MESH)

    @pl.loop(1, NG)
    def _(s):
        pl.semaphore_signal(barrier, inc=1, device_id=(lax.rem(g + s, NG), t), device_id_type=MESH)

    pltpu.make_async_copy(targets, wanted, tgt_sem).start()

    def batch(k):
        return k // 2

    def quantize(k, first, count):
        p, e = pair(k), batch(k)
        lane = lax.broadcasted_iota(jnp.int32, (1, QB), 1)
        tile = scales[e, g]
        for i in range(count):
            at = pl.multiple_of(p * CW + (first + i) * QB, QB)
            block = arrived[pl.ds(at, QB)].astype(jnp.float32)
            largest = jnp.max(jnp.abs(block), axis=(0, 1), keepdims=True)
            s = ((largest + 1e-06) / 448.0).astype(jnp.bfloat16).astype(jnp.float32)
            quant[rows(g), pl.ds(at, QB)] = (block / s).astype(jnp.bfloat16).T
            tile = jnp.where(lane == p * BLOCKS + first + i, jnp.broadcast_to(s, (1, QB)), tile)
        scales[e, g] = tile

    def send_own(k, at, width, early=False):
        block = quant.at[rows(g), pl.ds(pl.multiple_of(at, QB), width)]
        remote(block, block, own_send.at[0, k], early_recv.at[0] if early else prev_recv.at[k], (gn, t))
        remote(block, block, own_send.at[1, k], early_recv.at[1] if early else next_recv.at[k], (gp, t))
        remote(block, block, core_send.at[0, k], core_recv.at[0, k], (go, t))

    def send_scales(e):
        @pl.loop(1, NG)
        def _(s):
            remote(scales.at[e, g], scales.at[e, g], sc_send.at[e], sc_recv.at[e], (lax.rem(g + s, NG), t))

    pl.semaphore_wait(barrier, NT - 1 + NG - 1)

    def send_block(u):
        remote(panel.at[:, tens(u)], arrived.at[block_of(t)], a2a_send.at[u], a2a_recv.at[t], (g, u))

    def send_pair(j):
        dy, dx = shift(j)
        q = lax.rem(y + 4 - dy, 4) * 2 + lax.rem(xh + dx, 2)
        send_block(2 * q)
        send_block(2 * q + 1)

    other = 2 * p0 + 1 - odd
    edge = HALF + QB

    def columns(u, at, size):
        return pl.ds(pl.multiple_of(u * SRC + at, HALF), size)

    def near_part(u, side, first):
        at = (SRC - edge) * (1 - side) if first else edge * side
        return at, (edge if first else SRC - edge)

    for part in (True, False):
        at, size = near_part(t, odd, part)
        remote(
            panel.at[pl.ds(pl.multiple_of(at, HALF), size), tens(other)],
            arrived.at[columns(t, at, size)],
            near_send if part else a2a_send.at[other],
            near_recv if part else a2a_recv.at[t],
            (g, other),
        )

    for e in range(NP // 2):
        scales[e, g] = jnp.zeros((1, QB), jnp.float32)
    wait(arrived.at[block_of(t)], a2a_recv.at[t])
    quantize(0, 4 * odd, 3)
    send_own(0, p0 * CW + 4 * odd * QB, 3 * QB, early=True)
    for j in range(1, AHEAD):
        send_pair(j)
    pltpu.make_async_copy(hidden, states, hid_sem).start()
    logits[...] = jnp.zeros_like(logits)

    def forward(k, at):
        wait(quant.at[rows(gp), at], early_recv.at[0] if k is None else prev_recv.at[k])
        k0 = 0 if k is None else k
        top = quant.at[rows(gp, 0, HALF), at]
        remote(top, top, fwd_send.at[0, k0], top_recv.at[k0], (gn, t))
        wait(quant.at[rows(gn), at], early_recv.at[1] if k is None else next_recv.at[k])
        bot = quant.at[rows(gn, HALF, HALF), at]
        remote(bot, bot, fwd_send.at[1, k0], bot_recv.at[k0], (gp, t))

    def copy_near(k):
        for n, b in ((1, gp), (2, gn)):
            block = quant.at[rows(b), cols(pair(k))]
            remote(block, block, core_send.at[n, k], core_recv.at[n, k], (go, t))

    def step_near(k):
        forward(k, cols(pair(k)))
        copy_near(k)

    for part in (True, False):
        at, size = near_part(other, 1 - odd, part)
        wait(arrived.at[columns(other, at, size)], near_recv if part else a2a_recv.at[other])
        first = (3 - 1 * odd) if part else (5 - 5 * odd)
        quantize(0, first, 2)
        send_own(0, p0 * CW + first * QB, 2 * QB)

    forward(None, pl.ds(pl.multiple_of(p0 * CW + 4 * odd * QB, QB), 3 * QB))

    def step_own(k):
        p = pair(k)
        wait(arrived.at[block_of(2 * p)], a2a_recv.at[2 * p])
        wait(arrived.at[block_of(2 * p + 1)], a2a_recv.at[2 * p + 1])
        quantize(k, 0, BLOCKS)

        @pl.when(lax.rem(k, 2) == 1)
        def _():
            send_scales(batch(k))

        send_own(k, p * CW, CW)

    def step_far(k):
        p = pair(k)
        wait(quant.at[rows(gf, 0, HALF), cols(p)], top_recv.at[k])
        wait(quant.at[rows(gf, HALF, HALF), cols(p)], bot_recv.at[k])
        block = quant.at[rows(gf), cols(p)]
        remote(block, block, core_send.at[3, k], core_recv.at[3, k], (go, t))

    def dot(k, b):
        p = pair(k)
        both = []
        for h in range(2):
            s = pltpu.roll(scales[batch(k), 2 * b + h], lax.rem(QB - p * BLOCKS, QB), 1)
            spread = jnp.concatenate([jnp.broadcast_to(s[0:1, i:i + 1], (1, QB)) for i in range(BLOCKS)], axis=1)
            q = quant[rows(2 * b + h), cols(p)].astype(jnp.float32)
            both.append((q * spread).astype(jnp.bfloat16))
        w = jnp.concatenate(both, axis=0)
        at = pl.ds(pl.multiple_of(b * 256, 256), 256)
        logits[at, :] += lax.dot_general(
            w, states[:, cols(p)], (((1,), (1,)), ((), ())), preferred_element_type=jnp.float32
        )

    def dot_own(k):
        wait(quant.at[rows(0), cols(0)], core_recv.at[0, k])
        dot(k, z)

    def dot_near(k):
        for n in range(1, 3):
            wait(quant.at[rows(0), cols(0)], core_recv.at[n, k])

        @pl.loop(0, 2)
        def _(j):
            dot(k, lax.rem(z + 1 + 2 * j, NZ))

    def dot_far(k):
        wait(quant.at[rows(0), cols(0)], core_recv.at[3, k])
        dot(k, lax.rem(z + 2, NZ))

    p1 = pair(1)
    for first, count in ((0, 3), (3, 4)):
        source = 2 * p1 + first // 3
        wait(arrived.at[block_of(source)], a2a_recv.at[source])
        quantize(1, first, count)
        if first:
            send_scales(0)
        send_own(1, p1 * CW + first * QB, count * QB)
    send_pair(AHEAD)

    forward(0, pl.ds(pl.multiple_of(p0 * CW + (3 - 3 * odd) * QB, QB), 4 * QB))
    copy_near(0)
    for k in range(2, LEAD):
        send_pair(AHEAD - 1 + k)
        step_own(jnp.int32(k))

    @pl.loop(0, NP)
    def _(k):
        @pl.when(k < NP - (AHEAD - 1 + LEAD))
        def _():
            send_pair(k + AHEAD - 1 + LEAD)

        @pl.when(k < NP - LEAD)
        def _():
            step_own(k + LEAD)

        @pl.when(lax.rem(k, 2) == 1)
        def _():
            dot_own(k)

        @pl.when(k > 0)
        def _():
            step_near(k)

        @pl.when(k >= LAG)
        def _():
            step_far(k - LAG)

        @pl.when(k == 0)
        def _():
            pltpu.make_async_copy(hidden, states, hid_sem).wait()

        @pl.when(lax.rem(k, 2) == 0)
        def _():
            wait(scales.at[0, pl.ds(0, NG - 1)], sc_recv.at[batch(k)])
            dot_own(k)

        dot_near(k)

        @pl.when(k >= LAG)
        def _():
            dot_far(k - LAG)

    row = lax.broadcasted_iota(jnp.int32, (256, QB), 0)
    pltpu.make_async_copy(targets, wanted, tgt_sem).wait()

    def measure(b):
        @pl.loop(0, 8, unroll=4)
        def _(j):
            x = logits[pl.ds(pl.multiple_of(b * 256, 256), 256), pl.ds(pl.multiple_of(j * QB, QB), QB)]
            v = wanted[pl.ds(j, 1), :]
            mine = lax.rem(v // QB, NT) == t
            column = jnp.where(mine, v // (NT * QB) * QB + lax.rem(v, QB) - b * 256, -1)
            top = jnp.max(x, axis=0, keepdims=True)
            total = jnp.sum(jnp.exp(x - top), axis=0, keepdims=True)
            parts[b, 0, pl.ds(j, 1), :] = top + jnp.log(total)
            parts[b, 1, pl.ds(j, 1), :] = jnp.sum(jnp.where(row == column, x, 0.0), axis=0, keepdims=True)

    def combine(lses):
        top = jnp.max(lses, axis=0)
        return top + jnp.log(jnp.sum(jnp.exp(lses - top[None]), axis=0))

    for k in range(NP - LAG, NP - 2):
        step_far(k)
        dot_far(k)

    step_far(NP - 2)

    @pl.loop(0, 3)
    def _(j):
        measure(lax.rem(z + 3 + j, NZ))

    step_far(NP - 1)
    dot_far(NP - 2)
    dot_far(NP - 1)
    measure(lax.rem(z + 2, NZ))
    stats[t, 0] = combine(parts[:, 0])
    stats[t, 1] = jnp.sum(parts[:, 1], axis=0)

    @pl.loop(1, NT)
    def _(s):
        remote(stats.at[t], stats.at[t], st_send, st_recv, (g, lax.rem(t + s, NT)))

    table = jnp.concatenate([jnp.sum(scales[:, b], axis=0) for b in range(NG)], axis=0)
    scale[...] = table[:, :NP * BLOCKS].astype(jnp.bfloat16)

    wait(panel.at[pl.ds(0, edge), tens(0)], near_send)
    wait(panel.at[pl.ds(0, SRC - edge), tens(0)], a2a_send.at[other])

    @pl.loop(1, NP)
    def _(j):
        q = lax.rem(p0 + j, NP)
        wait(panel.at[:, tens(0)], a2a_send.at[2 * q])
        wait(panel.at[:, tens(0)], a2a_send.at[2 * q + 1])

    @pl.loop(0, NP)
    def _(k):
        chunk = quant.at[rows(0), cols(0)]
        half = quant.at[rows(0, 0, HALF), cols(0)]
        for n in range(2):
            wait(chunk, own_send.at[n, k])
            wait(half, fwd_send.at[n, k])
        for n in range(4):
            wait(chunk, core_send.at[n, k])

    for e in range(NP // 2):
        wait(scales.at[0, pl.ds(0, NG - 1)], sc_send.at[e])

    wait(stats.at[pl.ds(0, NT - 1)], st_recv)
    token = lax.broadcasted_iota(jnp.int32, (8, QB), 0) * QB + lax.broadcasted_iota(jnp.int32, (8, QB), 1)
    gap = jnp.sum(stats[:, 1], axis=0) - combine(stats[:, 0])
    logprob[...] = jnp.where(token < counts[0], gap, 0.0)
    wait(stats.at[pl.ds(0, NT - 1)], st_send)


def write(held, held_logprob, held_scale, quant, logprob, scale, sem):
    copies = [
        pltpu.make_async_copy(held.at[pl.ds(QB * i, QB)], quant.at[pl.ds(QB * i, QB)], sem.at[i]) for i in range(8)
    ]
    copies.append(pltpu.make_async_copy(held_logprob, logprob, sem.at[8]))
    copies.append(pltpu.make_async_copy(held_scale, scale, sem.at[9]))
    for copy in copies:
        copy.start()
    for copy in copies:
        copy.wait()


def local(panel, hidden, targets, counts):
    dma = pltpu.SemaphoreType.DMA
    vmem = pl.BlockSpec(memory_space=pltpu.VMEM)
    hbm = pl.BlockSpec(memory_space=pltpu.HBM)
    held = pl.pallas_call(
        kernel,
        out_shape=(
            pltpu.VMEM((8, QB), jnp.float32),
            pltpu.VMEM((ROWS, D), jnp.bfloat16),
            pltpu.VMEM((NG, NP * BLOCKS), jnp.bfloat16),
        ),
        in_specs=[hbm, hbm, hbm, pl.BlockSpec(memory_space=pltpu.SMEM)],
        out_specs=(vmem, vmem, vmem),
        scratch_shapes=[
            pltpu.VMEM((D, QB), jnp.bfloat16),
            pltpu.VMEM((ROWS, D), jnp.bfloat16),
            pltpu.VMEM((NP // 2, NG, 1, QB), jnp.float32),
            pltpu.VMEM((ROWS, ROWS), jnp.float32),
            pltpu.VMEM((8, QB), jnp.int32),
            pltpu.VMEM((NZ, 2, 8, QB), jnp.float32),
            pltpu.VMEM((NT, 2, 8, QB), jnp.float32),
            dma((NT,)), dma((NT,)), dma(()), dma(()), dma(()), dma(()),
            dma((2, NP)), dma((2, NP)), dma((4, NP)), dma((NP // 2,)), dma(()), dma((2,)),
            dma((NP,)), dma((NP,)), dma((NP,)), dma((NP,)), dma((4, NP)), dma((NP // 2,)), dma(()),
        ],
        compiler_params=pltpu.CompilerParams(
            collective_id=0, has_side_effects=True, vmem_limit_bytes=VMEM_LIMIT
        ),
        cost_estimate=pl.CostEstimate(
            flops=2 * ROWS * ROWS * D, bytes_accessed=4 * ROWS * D, transcendentals=ROWS * ROWS
        ),
        name="refresh",
    )(
        pltpu.with_memory_space_constraint(panel.T, pltpu.HBM),
        hidden,
        pltpu.with_memory_space_constraint(targets.reshape(8, QB), pltpu.HBM),
        counts,
    )
    quant, logprob, scale = pl.pallas_call(
        write,
        out_shape=(
            pltpu.HBM((ROWS, D), jnp.bfloat16),
            pltpu.HBM((8, QB), jnp.float32),
            pltpu.HBM((NG, NP * BLOCKS), jnp.bfloat16),
        ),
        in_specs=[vmem] * 3,
        out_specs=(hbm,) * 3,
        scratch_shapes=[dma((10,))],
        compiler_params=pltpu.CompilerParams(vmem_limit_bytes=2 << 20),
        cost_estimate=pl.CostEstimate(flops=0, bytes_accessed=4 * ROWS * D, transcendentals=0),
        name="write",
    )(held[1], held[0], held[2])
    return logprob.reshape(ROWS), quant, scale


def solution(mesh):
    in_specs = (P("group", "tensor"), P("group", None), P("group"), P("group"))
    out_specs = (P("group"), P("tensor", None), P("tensor", None))
    return jax.shard_map(local, mesh=mesh, in_specs=in_specs, out_specs=out_specs, check_vma=False)
```
